512 devices in a mesh: stream: 8 (over x, core), span: 8 (over z), depth: 8 (over y).
Axes of the slice: x: 4, y: 8, z: 8, core: 2. Of those that a mesh axis runs over, the one named last changes fastest.
Arguments:
- old_adjoint: float32 [3, 4096, 4096], P(None, ('stream', 'span', 'depth')), may hold values from -6 to 6
- target: int32 [4096], P(('stream', 'span', 'depth')), may hold values from 0 to 511, as said below
- velocity: bfloat16 [3, 128, 128, 1024], P(None, 'stream', 'span', 'depth'), may hold values from -3 to 3
- chi: float32 [128, 128, 1024], P('stream', 'span', 'depth'), may hold values from 0 to 1
- fish: int32 [8, 8, 64], P('stream', 'span', 'depth'), may hold values from 0 to 63
- fish_forcing: float32 [64, 3], replicated, may hold values from -6 to 6
Outputs:
- adjoint: float32 [3, 128, 128, 1024], P(None, 'stream', 'span', 'depth')
The draws below stay inside these ranges and needn't reach their ends.
Inputs may be any that keep to these rules, and one draw needn't show every extreme that they name: `target`: within each depth index, the 64 devices' entries name every number from 0 to 511 once. Each device sends its blocks to exactly 8 devices of its depth index, 1 block to each, and each device receives 1 block from each of 8 devices.
All inputs are finite; a program needn't handle non-finite values.
Results may differ from the reference program's by a relative error of at most 0.0003.
Values may be sent and summed in bfloat16 or wider, within the bound.
A program may use at most 64 MiB of HBM per device.

```python
import jax
import jax.numpy as jnp
from jax import lax

BLK = 16
BX_DEV = 1
BY_DEV = 1
BZ_DEV = 8
SECTIONS = 2
FISH = 64
B_DEV = 8
CELLS = 4096
GROUP = 64
PLANES = 8
CAP = 1
OLD_BLOCKS = 4096
XB = 8
YB = 8
ZB = 64
NX = 128
NY = 128
NZ = 1024
N_STREAM = 8
N_SPAN = 8


def draw_target(key, part):
    key = jax.random.fold_in(key, 11)

    def one_plane(plane_key):
        keys = jax.random.split(plane_key, 5)
        first = jax.random.permutation(keys[0], GROUP)
        second = jax.random.permutation(keys[1], GROUP)
        chosen = jax.random.permutation(keys[2], GROUP)[:B_DEV // CAP]
        offsets = jax.random.permutation(keys[3], jnp.repeat(chosen, CAP))
        owners = second[(first[:, None] + offsets[None, :]) % GROUP]
        orders = jax.vmap(lambda sub_key: jax.random.permutation(sub_key, B_DEV))(jax.random.split(keys[4], GROUP))
        slot_index = jnp.broadcast_to(jnp.arange(B_DEV)[None, :], (GROUP, B_DEV))
        local_slots = orders[owners, slot_index]
        return owners * B_DEV + local_slots
    planes = jax.vmap(one_plane)(jax.random.split(key, PLANES))
    return jnp.transpose(planes, (1, 0, 2)).reshape(-1).astype(jnp.int32)


def place_ends(result, own_key, smallest, top_value):
    index_at = [jax.random.randint(jax.random.fold_in(own_key, axis), (), 0, length) for axis, length in enumerate(result.shape)]
    main_axis = result.shape.index(max(result.shape))
    next_to = index_at[:main_axis] + [(index_at[main_axis] + 1) % result.shape[main_axis]] + index_at[main_axis + 1:]
    return result.at[tuple(index_at)].set(smallest).at[tuple(next_to)].set(top_value)


def block_scale(own_key, shape, pieces, smallest, largest):
    loudness = 1.0
    for dim, shards_of in pieces:
        steps = jax.random.uniform(jax.random.fold_in(jax.random.fold_in(own_key, 6), dim), (shards_of,), jnp.float32, smallest / len(pieces), largest / len(pieces))
        loudness = loudness * jnp.repeat(jnp.exp(steps), shape[dim] // shards_of).reshape((-1,) + (1,) * (len(shape) - 1 - dim))
    return loudness


def noise(stream_key, shape, scale, limit, pieces=(), held_as=jnp.bfloat16):
    drawn = scale * jax.random.normal(stream_key, shape, jnp.float32)
    if pieces:
        drawn = drawn * block_scale(stream_key, shape, pieces, -0.22, 0.18)
    return jnp.clip(drawn, -limit, limit).astype(held_as)


def setup_inputs(seed: int = 0) -> dict:
    streams_of = jax.random.split(jax.random.key(seed), 7)
    old_adjoint = noise(streams_of[0], (3, OLD_BLOCKS, CELLS), 1.0, 6.0, ((1, 512),), jnp.float32)
    target = draw_target(jax.random.fold_in(streams_of[6], 71), 0)
    velocity = noise(streams_of[2], (3, NX, NY, NZ), 0.5, 3.0, ((1, 8), (2, 8), (3, 8)))
    chi = jnp.clip(1.0 * jax.random.uniform(streams_of[3], (NX, NY, NZ), jnp.float32) ** block_scale(streams_of[3], (NX, NY, NZ), ((0, 8), (1, 8), (2, 8)), -0.2, 0.2), 0.0, 1.0)
    fish = place_ends(jax.random.randint(streams_of[4], (XB, YB, ZB), 0, FISH), jax.random.fold_in(streams_of[4], 1), 0, FISH - 1).astype(jnp.int32)
    fish_forcing = noise(streams_of[5], (FISH, 3), 1.0, 6.0, (), jnp.float32)
    return dict(old_adjoint=old_adjoint, target=target, velocity=velocity, chi=chi, fish=fish, fish_forcing=fish_forcing)


advect_coef = 0.1
diffuse_coef = 0.1


def interior(field):
    return field[:, 1:-1, 1:-1, 1:-1]


def offset(field, axis_num, shift_by):
    selection = [slice(None), slice(1, -1), slice(1, -1), slice(1, -1)]
    selection[axis_num] = slice(1 + shift_by, field.shape[axis_num] - 1 + shift_by)
    return field[tuple(selection)]


def centered(field, axis_num):
    return offset(field, axis_num, 1) - offset(field, axis_num, -1)


def advect(padded, carried, slopes):
    current = interior(padded)
    transport = carried[0:1] * centered(padded, 1) + carried[1:2] * centered(padded, 2) + carried[2:3] * centered(padded, 3)
    stretching = jnp.stack([jnp.sum(current * slopes[axis_num], axis=0) for axis_num in range(3)])
    return current + advect_coef * (transport - stretching)


def diffuse(padded):
    centre = interior(padded)
    total = offset(padded, 1, 1) + offset(padded, 1, -1)
    total = total + offset(padded, 2, 1) + offset(padded, 2, -1)
    total = total + offset(padded, 3, 1) + offset(padded, 3, -1)
    return centre + diffuse_coef * (total - 6.0 * centre)


def reference(old_adjoint, target, velocity, chi, fish, fish_forcing):
    old_blocks = old_adjoint.reshape(3, GROUP, PLANES, B_DEV, CELLS).transpose(0, 2, 1, 3, 4).reshape(3, PLANES, GROUP * B_DEV, CELLS)
    targets = target.reshape(GROUP, PLANES, B_DEV).transpose(1, 0, 2).reshape(PLANES, GROUP * B_DEV)

    def place_plane(blocks, wanted):
        return jnp.zeros_like(blocks).at[:, wanted].set(blocks)

    placed = jax.vmap(place_plane, in_axes=(1, 0), out_axes=1)(old_blocks, targets)
    field_now = placed.reshape(3, PLANES, N_STREAM, N_SPAN, BX_DEV, BY_DEV, BZ_DEV, BLK, BLK, BLK)
    field_now = field_now.transpose(0, 2, 4, 7, 3, 5, 8, 1, 6, 9).reshape(3, NX, NY, NZ)
    widths = ((0, 0), (2, 2), (2, 2), (2, 2))
    ghost_velocity = jnp.pad(velocity, widths)
    forcing_blocks = fish_forcing[fish]

    def one_section(current_field):
        padded = jnp.pad(current_field, widths)

        def one_plane(plane_num):
            a_slab = lax.dynamic_slice_in_dim(padded, plane_num, 5, 1)
            u_slab = lax.dynamic_slice_in_dim(ghost_velocity, plane_num, 5, 1).astype(jnp.float32)
            slopes = [centered(u_slab, axis_num) for axis_num in (1, 2, 3)]
            mixed_plane = diffuse(advect(a_slab, interior(u_slab), slopes))[:, 0]
            chi_plane = lax.dynamic_index_in_dim(chi, plane_num, 0, keepdims=False)
            block_row = lax.dynamic_index_in_dim(forcing_blocks, plane_num // BLK, 0, keepdims=False)
            forcing = jnp.repeat(jnp.repeat(jnp.moveaxis(block_row, 2, 0), BLK, axis=1), BLK, axis=2)
            return (mixed_plane + chi_plane[None] * forcing) / (1.0 + chi_plane[None])

        planes_out = lax.map(one_plane, jnp.arange(NX, dtype=jnp.int32))
        return jnp.moveaxis(planes_out, 0, 1)

    for section_num in range(SECTIONS):
        field_now = one_section(field_now)
    return field_now
```

```python
import functools

import jax
import jax.numpy as jnp
from jax import lax
from jax.experimental import pallas as pl
from jax.experimental.pallas import tpu as pltpu
from jax.sharding import PartitionSpec as P

SECTIONS = 2
ADVECT = 0.1
DIFFUSE = 0.1
LEVELS = 32767.0

RING = 8
CHIPS = 4
SLOTS = 8
EDGE = 16
TILES = 32
MESH = pl.DeviceIdType.MESH


def lanes_of(shape):
    return lax.broadcasted_iota(jnp.int32, shape, len(shape) - 1)


def rows_of(shape):
    return lax.broadcasted_iota(jnp.int32, shape, len(shape) - 2)


def swap_groups(tile):
    row, group = rows_of(tile.shape), lanes_of(tile.shape) // EDGE
    for bit in (1, 2, 4):
        row_bit, group_bit = (row & bit) != 0, (group & bit) != 0
        down = pltpu.roll(pltpu.roll(tile, bit, 0), 128 - EDGE * bit, 1)
        if bit == 4:
            up = down
        else:
            up = pltpu.roll(pltpu.roll(tile, 8 - bit, 0), EDGE * bit, 1)
        tile = jnp.where(row_bit == group_bit, tile, jnp.where(row_bit, down, up))
    return tile


def pack_ends(tiles):
    pair = ((lanes_of((8, 128)) + 1) & 127) // 2
    shift = 1
    while len(tiles) > 1:
        later = (pair & shift) != 0
        tiles = [
            jnp.where(later, pltpu.roll(b, 2 * shift, 1), a)
            for a, b in zip(tiles[0::2], tiles[1::2])
        ]
        shift *= 2
    return tiles[0]


def kernel(
    target, fish, forcing, old, velocity, chi, out,
    gathered, meta, staged, outgoing, out_scales, incoming, in_scales, decoded,
    found, found_s, fields, face_y, halo_y, face_z, halo_z, slopes, weight, pull,
    send_sems, recv_sems, local_sem,
):
    stream, span, depth = (lax.axis_index(a) for a in ("stream", "span", "depth"))
    chip, core = stream // 2, stream % 2
    other_core = {"stream": chip * 2 + 1 - core}

    def along(axis, index, step):
        return {axis: (index + step + RING) % RING}

    copies = {}

    def send(key, src, dst, device):
        number = len(copies)
        copy = pltpu.make_async_remote_copy(
            src_ref=src,
            dst_ref=dst,
            send_sem=send_sems.at[number],
            recv_sem=recv_sems.at[number],
            device_id=device,
            device_id_type=MESH,
        )
        copies[key] = copy
        copy.start()

    barrier = pltpu.get_barrier_semaphore()
    partners = [along("span", span, 1), along("span", span, -1)]
    partners += [along("depth", depth, 1), along("depth", depth, -1)]
    partners += [along("stream", stream, s) for s in (1, -1, 2, 4, 6)]
    for partner in partners:
        pl.semaphore_signal(barrier, inc=1, device_id=partner, device_id_type=MESH)

    for c in range(3):
        top = jnp.abs(old[c, :, 0:128])
        for t in range(1, TILES):
            top = jnp.maximum(top, jnp.abs(old[c, :, 128 * t : 128 * t + 128]))
        meta[0, c] = top * (1.0 / LEVELS)
        inverse = LEVELS / jnp.maximum(top, 1e-30)
        for t in range(TILES):
            staged[c][pl.ds(t, SLOTS, stride=TILES), :] = jnp.round(
                old[c, :, 128 * t : 128 * t + 128] * inverse
            )
        for b in range(SLOTS):
            codes = staged[c][TILES * b : TILES * (b + 1), :]
            gathered[c][b] = codes.astype(jnp.int32).astype(jnp.int16)
    label = jnp.zeros((8, 128), jnp.int32)
    for b in range(SLOTS):
        label = jnp.where(rows_of((8, 128)) == b, target[b], label)
    meta[0, 3] = label.astype(jnp.float32)

    pl.semaphore_wait(barrier, len(partners))

    def places(kind, e, part):
        if kind == 3:
            return meta.at[e]
        if part is None:
            return gathered[kind].at[pl.ds(8 * e, 8)]
        return gathered[kind].at[pl.ds(8 * e + 4 * part, 4)]

    def hop_right(kind, hop):
        part = 0 if hop == 4 and kind < 3 else None
        send(("r", kind, hop), places(kind, hop - 1, part), places(kind, hop, part), along("span", span, 1))

    def hop_left(kind, hop):
        part = 1 if hop == 4 else None
        send(("l", kind, hop), places(kind, (9 - hop) % 8, part), places(kind, 8 - hop, part), along("span", span, -1))

    def to_core(kind, e, part=None):
        send(("c", kind, e, part), places(kind, e, part), places(kind, 8 + e, part), other_core)

    kinds = (3, 0, 1, 2)
    for kind in kinds:
        hop_right(kind, 1)
        hop_left(kind, 1)
    for kind in kinds:
        to_core(kind, 0)

    def keep_faces(n, i, c, value):
        face_y[n][0, i * 3 + c : i * 3 + c + 1, :] = value[0:1]
        face_y[n][1, i * 3 + c : i * 3 + c + 1, :] = value[EDGE - 1 : EDGE]

    def keep_ends(n, tiles):
        for c in range(3):
            face_z[n][c] = pack_ends(tiles[c])

    def start_halo(n):
        field = fields[n]
        send((n, "x", 0), field.at[pl.ds(48, 3)], field.at[pl.ds(0, 3)], along("stream", stream, 1))
        send((n, "x", 1), field.at[pl.ds(3, 3)], field.at[pl.ds(51, 3)], along("stream", stream, -1))
        send((n, "y", 0), face_y[n].at[1], halo_y[n].at[0], along("span", span, 1))
        send((n, "y", 1), face_y[n].at[0], halo_y[n].at[1], along("span", span, -1))
        send((n, "z", 0), face_z[n], halo_z[n].at[0], along("depth", depth, 1))
        send((n, "z", 1), face_z[n], halo_z[n].at[1], along("depth", depth, -1))

    def finish_halo(n):
        for axis in ("x", "y", "z"):
            for side in (0, 1):
                copies[(n, axis, side)].wait_recv()

        @pl.when(stream == 0)
        def _():
            fields[n][0:3] = jnp.zeros((3, EDGE, 128), jnp.float32)

        @pl.when(stream == RING - 1)
        def _():
            fields[n][51:54] = jnp.zeros((3, EDGE, 128), jnp.float32)

        @pl.when(span == 0)
        def _():
            halo_y[n][0] = jnp.zeros((48, 128), jnp.float32)

        @pl.when(span == RING - 1)
        def _():
            halo_y[n][1] = jnp.zeros((48, 128), jnp.float32)

        ends = []
        odd = (lanes_of((8, 128)) & 1) == 1
        for c in range(3):
            before = jnp.where(depth == 0, 0.0, pltpu.roll(halo_z[n][0, c], 1, 1))
            after = jnp.where(depth == RING - 1, 0.0, pltpu.roll(halo_z[n][1, c], 127, 1))
            ends.append(jnp.where(odd, after, before))
        return ends

    wide = (EDGE, 128)

    def around(n, ends, i, c):
        here = fields[n][(i + 1) * 3 + c]
        row, lane = rows_of(wide), lanes_of(wide)
        at = i * 3 + c
        y_before = jnp.where(row == 0, halo_y[n][0, at : at + 1, :], pltpu.roll(here, 1, 0))
        y_after = jnp.where(row == EDGE - 1, halo_y[n][1, at : at + 1, :], pltpu.roll(here, EDGE - 1, 0))
        end = jnp.concatenate(
            [pltpu.roll(ends[c], (128 - 2 * v) % 128, 1) for v in (2 * i, 2 * i + 1)], axis=0
        )
        z_before = jnp.where(lane == 0, end, pltpu.roll(here, 1, 1))
        z_after = jnp.where(lane == 127, end, pltpu.roll(here, 127, 1))
        return here, fields[n][i * 3 + c], fields[n][(i + 2) * 3 + c], y_before, y_after, z_before, z_after

    tiles = [[], [], []]
    for i in range(EDGE):
        for c in range(3):
            value = velocity[c, i].astype(jnp.float32)
            fields[4][(i + 1) * 3 + c] = value
            keep_faces(4, i, c, value)
            tiles[c] += [value[0:8], value[8:16]]
    keep_ends(4, tiles)
    start_halo(4)

    def forward(kind, hop):
        copies[("r", kind, hop)].wait_recv()
        if hop < 4:
            hop_right(kind, hop + 1)
        if hop < 4 or kind == 3:
            to_core(kind, hop)
        else:
            to_core(kind, hop, 0)
        if hop == 4 and kind == 3:
            return
        copies[("l", kind, hop)].wait_recv()
        if hop < 3 or kind < 3 and hop == 3:
            hop_left(kind, hop + 1)
        if hop < 4:
            to_core(kind, 8 - hop)
        else:
            to_core(kind, 4, 1)

    for kind in kinds:
        forward(kind, 1)

    ends = finish_halo(4)
    for i in range(EDGE):
        for k in range(3):
            _, *near = around(4, ends, i, k)
            for axis in range(3):
                slopes[(axis * 3 + k) * EDGE + i] = ADVECT * (near[2 * axis + 1] - near[2 * axis])

    for kind in kinds:
        forward(kind, 2)

    group = lanes_of(wide) // EDGE
    forces = []
    for c in range(3):
        force = jnp.zeros(wide, jnp.float32)
        for b in range(SLOTS):
            force = jnp.where(group == b, forcing[fish[0, 0, b], c], force)
        forces.append(force)
    for i in range(EDGE):
        level = chi[i]
        share = 1.0 / (1.0 + level)
        weight[i] = share
        for c in range(3):
            pull[i * 3 + c] = level * share * forces[c]

    for kind in kinds:
        forward(kind, 3)
    forward(3, 4)
    for e in range(8):
        copies[("c", 3, e, None)].wait_recv()

    shape = (8, 128)
    lane, row = lanes_of(shape), rows_of(shape)
    owner = (2 * ((chip + lane // 8) % CHIPS) + core) * RING + span
    wanted = jnp.where(lane < CHIPS * SLOTS, owner * SLOTS + lane % 8, -1).astype(jnp.float32)
    at = jnp.zeros(shape, jnp.float32)
    for e in range(16):
        at = at + jnp.where(meta[e, 3] == wanted, (row + (8 * e + 1)).astype(jnp.float32), 0.0)
    found[...] = jnp.broadcast_to(jnp.sum(at, axis=0, keepdims=True), shape).astype(jnp.int32)
    copy = pltpu.make_async_copy(found, found_s, local_sem)
    copy.start()
    copy.wait()
    where_from = []
    for q in range(CHIPS * SLOTS):
        k, j = q // SLOTS, q % SLOTS
        code = found_s[0, q]
        block = jnp.minimum(jnp.maximum(code - 1, 0), 127)
        where_from.append(block)
        valid = jnp.where(code > 0, 1.0, 0.0)
        for c in range(3):
            scale = meta[block // 8, c, pl.ds(block % 8, 1), :] * valid
            if k == 0:
                in_scales[0, c, j : j + 1, :] = scale
            else:
                out_scales[k - 1, c, j : j + 1, :] = scale
    for k in (2, 1, 3):
        send(("s", k), out_scales.at[k - 1], in_scales.at[k], along("stream", stream, 2 * k))

    for kind in (0, 1, 2):
        forward(kind, 4)
        for e in range(8):
            for part in (0, 1) if e == 4 else (None,):
                copies[("c", kind, e, part)].wait_recv()
        for k in (2, 1, 3, 0):
            for j in range(SLOTS):
                block = gathered[kind][where_from[k * SLOTS + j]]
                if k == 0:
                    incoming[kind][0, j] = block
                else:
                    outgoing[kind][k - 1, j] = block
            if k:
                send(("x", kind, k), outgoing[kind].at[k - 1], incoming[kind].at[k], along("stream", stream, 2 * k))

    for k in (2, 1, 3):
        copies[("s", k)].wait_recv()
    tiles = [[], [], []]
    for c in range(3):
        for k in (2, 1, 3):
            copies[("x", c, k)].wait_recv()
        for j in range(SLOTS):
            total = incoming[c][0, j].astype(jnp.float32) * in_scales[0, c, j : j + 1, :]
            for k in range(1, CHIPS):
                total = total + incoming[c][k, j].astype(jnp.float32) * in_scales[k, c, j : j + 1, :]
            decoded[c][TILES * j : TILES * (j + 1), :] = total
        for i in range(EDGE):
            halves = [swap_groups(decoded[c][pl.ds(2 * i + h, SLOTS, stride=TILES), :]) for h in (0, 1)]
            for h in (0, 1):
                fields[0][(i + 1) * 3 + c, 8 * h : 8 * h + 8, :] = halves[h]
            face_y[0][0, i * 3 + c : i * 3 + c + 1, :] = halves[0][0:1]
            face_y[0][1, i * 3 + c : i * 3 + c + 1, :] = halves[1][7:8]
            tiles[c] += halves
    keep_ends(0, tiles)

    for section in range(SECTIONS):
        n = 2 * section
        start_halo(n)
        ends = finish_halo(n)
        tiles = [[], [], []]
        for i in range(EDGE):
            near = [around(n, ends, i, c) for c in range(3)]
            carried = [ADVECT * fields[4][(i + 1) * 3 + k] for k in range(3)]
            for c in range(3):
                value = near[c][0]
                for k in range(3):
                    value = value + carried[k] * (near[c][2 * k + 2] - near[c][2 * k + 1])
                    value = value - near[k][0] * slopes[(c * 3 + k) * EDGE + i]
                fields[n + 1][(i + 1) * 3 + c] = value
                keep_faces(n + 1, i, c, value)
                tiles[c] += [value[0:8], value[8:16]]
        keep_ends(n + 1, tiles)
        start_halo(n + 1)
        ends = finish_halo(n + 1)
        tiles = [[], [], []]
        for i in range(EDGE):
            share = weight[i]
            for c in range(3):
                here, *near = around(n + 1, ends, i, c)
                total = (near[0] + near[1]) + (near[2] + near[3]) + (near[4] + near[5])
                value = (here + DIFFUSE * (total - 6.0 * here)) * share + pull[i * 3 + c]
                if section == SECTIONS - 1:
                    out[c, i] = value
                else:
                    fields[n + 2][(i + 1) * 3 + c] = value
                    keep_faces(n + 2, i, c, value)
                    tiles[c] += [value[0:8], value[8:16]]
        if section < SECTIONS - 1:
            keep_ends(n + 2, tiles)

    for copy in copies.values():
        copy.wait_send()


def body(old_adjoint, target, velocity, chi, fish, fish_forcing):
    f32, i16 = jnp.float32, jnp.int16
    v = pltpu.VMEM
    scratch = [
        [v((128, TILES, 128), i16)] * 3,
        v((16, 4, 8, 128), f32),
        [v((SLOTS * TILES, 128), f32)] * 3,
        [v((CHIPS - 1, SLOTS, TILES, 128), i16)] * 3,
        v((CHIPS - 1, 3, SLOTS, 128), f32),
        [v((CHIPS, SLOTS, TILES, 128), i16)] * 3,
        v((CHIPS, 3, SLOTS, 128), f32),
        [v((SLOTS * TILES, 128), f32)] * 3,
        v((8, 128), jnp.int32),
        pltpu.SMEM((8, 128), jnp.int32),
        [v((18 * 3, EDGE, 128), f32)] * 5,
        [v((2, 48, 128), f32)] * 5,
        [v((2, 48, 128), f32)] * 5,
        [v((3, 8, 128), f32)] * 5,
        [v((2, 3, 8, 128), f32)] * 5,
        v((9 * EDGE, EDGE, 128), f32),
        v((EDGE, EDGE, 128), f32),
        v((3 * EDGE, EDGE, 128), f32),
        pltpu.SemaphoreType.DMA((128,)),
        pltpu.SemaphoreType.DMA((128,)),
        pltpu.SemaphoreType.DMA,
    ]
    smem = pl.BlockSpec(memory_space=pltpu.SMEM)
    vmem = pl.BlockSpec(memory_space=pltpu.VMEM)
    return pl.pallas_call(
        kernel,
        out_shape=jax.ShapeDtypeStruct(velocity.shape, f32),
        in_specs=[smem, smem, smem, vmem, vmem, vmem],
        out_specs=vmem,
        scratch_shapes=scratch,
        compiler_params=pltpu.CompilerParams(
            collective_id=0, has_side_effects=True, vmem_limit_bytes=40 * 1024 * 1024
        ),
    )(target, fish, fish_forcing, old_adjoint, velocity, chi)


def solution(mesh):
    return jax.shard_map(
        body,
        mesh=mesh,
        in_specs=(
            P(None, ("stream", "span", "depth"), None),
            P(("stream", "span", "depth")),
            P(None, "stream", "span", "depth"),
            P("stream", "span", "depth"),
            P("stream", "span", "depth"),
            P(),
        ),
        out_specs=P(None, "stream", "span", "depth"),
        check_vma=False,
    )
```

```python
import functools

import jax
import jax.numpy as jnp
from jax import lax
from jax.experimental import pallas as pl
from jax.experimental.pallas import tpu as pltpu
from jax.sharding import PartitionSpec as P

SECTIONS = 2
ADVECT = 0.1
DIFFUSE = 0.1
LEVELS = 32767.0

RING = 8
CHIPS = 4
SLOTS = 8
EDGE = 16
PARTS = 6
TILES = 16
LAST = 7
MESH = pl.DeviceIdType.MESH


def lanes_of(shape):
    return lax.broadcasted_iota(jnp.int32, shape, len(shape) - 1)


def rows_of(shape):
    return lax.broadcasted_iota(jnp.int32, shape, len(shape) - 2)


def swap_groups(tiles):
    row, group = rows_of((8, 128)), lanes_of((8, 128)) // EDGE
    for bit in (1, 2, 4):
        row_bit, group_bit = (row & bit) != 0, (group & bit) != 0
        same, moved = row_bit == group_bit, []
        for tile in tiles:
            down = pltpu.roll(pltpu.roll(tile, bit, 0), 128 - EDGE * bit, 1)
            up = down
            if bit != 4:
                up = pltpu.roll(pltpu.roll(tile, 8 - bit, 0), EDGE * bit, 1)
            moved.append(jnp.where(same, tile, jnp.where(row_bit, down, up)))
        tiles = moved
    return tiles


def pack_ends(tiles):
    pair = ((lanes_of((8, 128)) + 1) & 127) // 2
    shift = 1
    while len(tiles) > 1:
        later = (pair & shift) != 0
        tiles = [
            jnp.where(later, pltpu.roll(b, 2 * shift, 1), a)
            for a, b in zip(tiles[0::2], tiles[1::2])
        ]
        shift *= 2
    return tiles[0]


def kernel(
    target, fish, forcing, old_far, velocity_far, chi_far, out, old, velocity, chi,
    gathered, meta, staged, outgoing, out_scales, incoming, in_scales, decoded,
    found, found_s, fields, face_y, halo_y, face_z, halo_z, slopes, weight, pull,
    send_sems, recv_sems, local_sems,
):
    stream, span, depth = (lax.axis_index(a) for a in ("stream", "span", "depth"))
    chip, core = stream // 2, stream % 2
    other_core = {"stream": chip * 2 + 1 - core}

    def along(axis, index, step):
        return {axis: (index + step + RING) % RING}

    copies = {}

    def send(key, src, dst, device):
        number = len(copies)
        copy = pltpu.make_async_remote_copy(
            src_ref=src,
            dst_ref=dst,
            send_sem=send_sems.at[number],
            recv_sem=recv_sems.at[number],
            device_id=device,
            device_id_type=MESH,
        )
        copies[key] = copy
        copy.start()

    fetched = [
        pltpu.make_async_copy(src, dst, local_sems.at[i])
        for i, (src, dst) in enumerate(((old_far, old), (velocity_far, velocity), (chi_far, chi)))
    ]
    for copy in fetched:
        copy.start()

    barrier = pltpu.get_barrier_semaphore()
    partners = [along("span", span, 1), along("span", span, -1)]
    partners += [along("depth", depth, 1), along("depth", depth, -1)]
    partners += [along("stream", stream, s) for s in (1, -1, 2, 4, 6)]
    for partner in partners:
        pl.semaphore_signal(barrier, inc=1, device_id=partner, device_id_type=MESH)

    fetched[0].wait()
    tops = [jnp.abs(old[c, :, 0:128]) for c in range(3)]
    for t in range(1, 2 * TILES):
        for c in range(3):
            tops[c] = jnp.maximum(tops[c], jnp.abs(old[c, :, 128 * t : 128 * t + 128]))
    top = jnp.maximum(jnp.maximum(tops[0], tops[1]), tops[2])
    meta[0, 0] = top * (1.0 / LEVELS)
    inverse = LEVELS / jnp.maximum(top, 1e-30)
    for kind in range(PARTS):
        c, first = kind // 2, kind % 2 * TILES
        for t in range(TILES):
            begin = 128 * (first + t)
            staged[kind][pl.ds(t, SLOTS, stride=TILES), :] = jnp.round(old[c, :, begin : begin + 128] * inverse)
        for b in range(SLOTS):
            codes = staged[kind][TILES * b : TILES * (b + 1), :]
            gathered[kind][b] = codes.astype(jnp.int32).astype(jnp.int16)
    label = jnp.zeros((8, 128), jnp.int32)
    for b in range(SLOTS):
        label = jnp.where(rows_of((8, 128)) == b, target[b], label)
    meta[0, 1] = label.astype(jnp.float32)

    pl.semaphore_wait(barrier, len(partners))

    def places(kind, place, count=8, skip=0):
        if kind == PARTS:
            return meta.at[pl.ds(place, count // 8)]
        return gathered[kind].at[pl.ds(8 * place + skip, count)]

    def hop_right(kind, hop):
        source = max(2 * hop - 3, 0)
        count = 4 if hop == 4 and kind < PARTS else 8
        send(("r", kind, hop), places(kind, source, count), places(kind, 2 * hop - 1, count), along("span", span, 1))

    def hop_left(kind, hop):
        source, to, count, skip = 2 * hop - 2, 2 * hop, 8, 0
        if hop == 4:
            to, count, skip = LAST, 4, 4
        send(("l", kind, hop), places(kind, source, count, skip), places(kind, to, count, skip), along("span", span, -1))

    def to_core(kind, hop):
        first = max(2 * hop - 1, 0)
        count = 8 if hop in (0, 4) else 16
        send(("c", kind, hop), places(kind, first, count), places(kind, 8 + first, count), other_core)

    kinds = (0, PARTS, *range(1, PARTS))
    for kind in kinds:
        hop_right(kind, 1)
        hop_left(kind, 1)
    for kind in kinds:
        to_core(kind, 0)

    def keep_faces(n, i, c, value):
        face_y[n][0, i * 3 + c : i * 3 + c + 1, :] = value[0:1]
        face_y[n][1, i * 3 + c : i * 3 + c + 1, :] = value[EDGE - 1 : EDGE]

    def keep_ends(n, tiles):
        for c in range(3):
            face_z[n][c] = pack_ends(tiles[c])

    def start_halo(n):
        field = fields[n]
        send((n, "x", 0), field.at[pl.ds(48, 3)], field.at[pl.ds(0, 3)], along("stream", stream, 1))
        send((n, "x", 1), field.at[pl.ds(3, 3)], field.at[pl.ds(51, 3)], along("stream", stream, -1))
        send((n, "y", 0), face_y[n].at[1], halo_y[n].at[0], along("span", span, 1))
        send((n, "y", 1), face_y[n].at[0], halo_y[n].at[1], along("span", span, -1))
        send((n, "z", 0), face_z[n], halo_z[n].at[0], along("depth", depth, 1))
        send((n, "z", 1), face_z[n], halo_z[n].at[1], along("depth", depth, -1))

    def finish_halo(n):
        for axis in ("x", "y", "z"):
            for side in (0, 1):
                copies[(n, axis, side)].wait_recv()

        @pl.when(stream == 0)
        def _():
            fields[n][0:3] = jnp.zeros((3, EDGE, 128), jnp.float32)

        @pl.when(stream == RING - 1)
        def _():
            fields[n][51:54] = jnp.zeros((3, EDGE, 128), jnp.float32)

        @pl.when(span == 0)
        def _():
            halo_y[n][0] = jnp.zeros((48, 128), jnp.float32)

        @pl.when(span == RING - 1)
        def _():
            halo_y[n][1] = jnp.zeros((48, 128), jnp.float32)

        ends = []
        odd = (lanes_of((8, 128)) & 1) == 1
        for c in range(3):
            before = jnp.where(depth == 0, 0.0, pltpu.roll(halo_z[n][0, c], 1, 1))
            after = jnp.where(depth == RING - 1, 0.0, pltpu.roll(halo_z[n][1, c], 127, 1))
            ends.append(jnp.where(odd, after, before))
        return ends

    wide = (EDGE, 128)

    def around(n, ends, i, c):
        here = fields[n][(i + 1) * 3 + c]
        row, lane = rows_of(wide), lanes_of(wide)
        at = i * 3 + c
        y_before = jnp.where(row == 0, halo_y[n][0, at : at + 1, :], pltpu.roll(here, 1, 0))
        y_after = jnp.where(row == EDGE - 1, halo_y[n][1, at : at + 1, :], pltpu.roll(here, EDGE - 1, 0))
        end = jnp.concatenate(
            [pltpu.roll(ends[c], (128 - 2 * v) % 128, 1) for v in (2 * i, 2 * i + 1)], axis=0
        )
        z_before = jnp.where(lane == 0, end, pltpu.roll(here, 1, 1))
        z_after = jnp.where(lane == 127, end, pltpu.roll(here, 127, 1))
        return here, fields[n][i * 3 + c], fields[n][(i + 2) * 3 + c], y_before, y_after, z_before, z_after

    fetched[1].wait()
    tiles = [[], [], []]
    for i in range(EDGE):
        for c in range(3):
            value = velocity[c, i].astype(jnp.float32)
            fields[4][(i + 1) * 3 + c] = value
            keep_faces(4, i, c, value)
            tiles[c] += [value[0:8], value[8:16]]
    keep_ends(4, tiles)
    start_halo(4)

    def forward(kind, hop):
        copies[("r", kind, hop)].wait_recv()
        if hop < 4:
            hop_right(kind, hop + 1)
        if hop < 4 or kind < PARTS:
            copies[("l", kind, hop)].wait_recv()
        if hop < 3 or hop == 3 and kind < PARTS:
            hop_left(kind, hop + 1)
        to_core(kind, hop)

    for kind in kinds:
        forward(kind, 1)

    ends = finish_halo(4)
    for i in range(EDGE):
        for k in range(3):
            _, *near = around(4, ends, i, k)
            for axis in range(3):
                slopes[(axis * 3 + k) * EDGE + i] = ADVECT * (near[2 * axis + 1] - near[2 * axis])

    for kind in kinds:
        forward(kind, 2)

    fetched[2].wait()
    group = lanes_of(wide) // EDGE
    forces = []
    for c in range(3):
        force = jnp.zeros(wide, jnp.float32)
        for b in range(SLOTS):
            force = jnp.where(group == b, forcing[c, fish[0, 0, b]], force)
        forces.append(force)
    for i in range(EDGE):
        level = chi[i]
        share = 1.0 / (1.0 + level)
        weight[i] = share
        for c in range(3):
            pull[i * 3 + c] = level * share * forces[c]

    for kind in kinds:
        forward(kind, 3)
    forward(PARTS, 4)
    for hop in range(5):
        copies[("c", PARTS, hop)].wait_recv()

    shape = (8, 128)
    lane, row = lanes_of(shape), rows_of(shape)
    owner = (2 * ((chip + lane // 8) % CHIPS) + core) * RING + span
    wanted = jnp.where(lane < CHIPS * SLOTS, owner * SLOTS + lane % 8, -1).astype(jnp.float32)
    at = jnp.zeros(shape, jnp.float32)
    for e in range(16):
        at = at + jnp.where(meta[e, 1] == wanted, (row + (8 * e + 1)).astype(jnp.float32), 0.0)
    found[...] = jnp.broadcast_to(jnp.sum(at, axis=0, keepdims=True), shape).astype(jnp.int32)
    copy = pltpu.make_async_copy(found, found_s, local_sems.at[3])
    copy.start()
    copy.wait()
    where_from = []
    for q in range(CHIPS * SLOTS):
        k, j = q // SLOTS, q % SLOTS
        code = found_s[0, q]
        block = jnp.minimum(jnp.maximum(code - 1, 0), 127)
        where_from.append(block)
        scale = meta[block >> 3, 0, pl.ds(block & 7, 1), :] * jnp.where(code > 0, 1.0, 0.0)
        if k == 0:
            in_scales[0, j : j + 1, :] = scale
        else:
            out_scales[k - 1, j : j + 1, :] = scale
    for k in (2, 1, 3):
        send(("s", k), out_scales.at[k - 1], in_scales.at[k], along("stream", stream, 2 * k))

    def pick(kind):
        for hop in range(5):
            copies[("c", kind, hop)].wait_recv()
        for k in (2, 1, 3, 0):
            for j in range(SLOTS):
                block = gathered[kind][where_from[k * SLOTS + j]]
                if k == 0:
                    incoming[kind][0, j] = block
                else:
                    outgoing[kind][k - 1, j] = block
            if k:
                send(("x", kind, k), outgoing[kind].at[k - 1], incoming[kind].at[k], along("stream", stream, 2 * k))

    for kind in range(PARTS):
        forward(kind, 4)
        if kind:
            pick(kind - 1)
    pick(PARTS - 1)

    for k in (2, 1, 3):
        copies[("s", k)].wait_recv()
    tiles = [[], [], []]
    for kind in range(PARTS):
        c, first = kind // 2, kind % 2 * (EDGE // 2)
        for k in (2, 1, 3):
            copies[("x", kind, k)].wait_recv()
        for j in range(SLOTS):
            total = incoming[kind][0, j].astype(jnp.float32) * in_scales[0, j : j + 1, :]
            for k in range(1, CHIPS):
                total = total + incoming[kind][k, j].astype(jnp.float32) * in_scales[k, j : j + 1, :]
            decoded[kind][TILES * j : TILES * (j + 1), :] = total
        moved = swap_groups([decoded[kind][pl.ds(t, SLOTS, stride=TILES), :] for t in range(TILES)])
        tiles[c] += moved
        for t, tile in enumerate(moved):
            i, h = first + t // 2, t % 2
            fields[0][(i + 1) * 3 + c, 8 * h : 8 * h + 8, :] = tile
            face_y[0][h, i * 3 + c : i * 3 + c + 1, :] = tile[7 * h : 7 * h + 1]
    keep_ends(0, tiles)

    for section in range(SECTIONS):
        n = 2 * section
        start_halo(n)
        ends = finish_halo(n)
        tiles = [[], [], []]
        for i in range(EDGE):
            near = [around(n, ends, i, c) for c in range(3)]
            carried = [ADVECT * fields[4][(i + 1) * 3 + k] for k in range(3)]
            for c in range(3):
                value = near[c][0]
                for k in range(3):
                    value = value + carried[k] * (near[c][2 * k + 2] - near[c][2 * k + 1])
                    value = value - near[k][0] * slopes[(c * 3 + k) * EDGE + i]
                fields[n + 1][(i + 1) * 3 + c] = value
                keep_faces(n + 1, i, c, value)
                tiles[c] += [value[0:8], value[8:16]]
        keep_ends(n + 1, tiles)
        start_halo(n + 1)
        ends = finish_halo(n + 1)
        tiles = [[], [], []]
        for i in range(EDGE):
            share = weight[i]
            for c in range(3):
                here, *near = around(n + 1, ends, i, c)
                total = (near[0] + near[1]) + (near[2] + near[3]) + (near[4] + near[5])
                value = (here + DIFFUSE * (total - 6.0 * here)) * share + pull[i * 3 + c]
                if section == SECTIONS - 1:
                    out[c, i] = value
                else:
                    fields[n + 2][(i + 1) * 3 + c] = value
                    keep_faces(n + 2, i, c, value)
                    tiles[c] += [value[0:8], value[8:16]]
        if section < SECTIONS - 1:
            keep_ends(n + 2, tiles)

    for copy in copies.values():
        copy.wait_send()


def body(old_adjoint, target, velocity, chi, fish, fish_forcing):
    f32, i16 = jnp.float32, jnp.int16
    v = pltpu.VMEM
    scratch = [
        v((3, SLOTS, 2 * TILES * 128), f32),
        v(velocity.shape, velocity.dtype),
        v(chi.shape, f32),
        [v((128, TILES, 128), i16)] * PARTS,
        v((16, 2, 8, 128), f32),
        [v((SLOTS * TILES, 128), f32)] * PARTS,
        [v((CHIPS - 1, SLOTS, TILES, 128), i16)] * PARTS,
        v((CHIPS - 1, SLOTS, 128), f32),
        [v((CHIPS, SLOTS, TILES, 128), i16)] * PARTS,
        v((CHIPS, SLOTS, 128), f32),
        [v((SLOTS * TILES, 128), f32)] * PARTS,
        v((8, 128), jnp.int32),
        pltpu.SMEM((8, 128), jnp.int32),
        [v((18 * 3, EDGE, 128), f32)] * 5,
        [v((2, 48, 128), f32)] * 5,
        [v((2, 48, 128), f32)] * 5,
        [v((3, 8, 128), f32)] * 5,
        [v((2, 3, 8, 128), f32)] * 5,
        v((9 * EDGE, EDGE, 128), f32),
        v((EDGE, EDGE, 128), f32),
        v((3 * EDGE, EDGE, 128), f32),
        pltpu.SemaphoreType.DMA((192,)),
        pltpu.SemaphoreType.DMA((192,)),
        pltpu.SemaphoreType.DMA((4,)),
    ]
    smem = pl.BlockSpec(memory_space=pltpu.SMEM)
    far = pl.BlockSpec(memory_space=pl.ANY)
    vmem = pl.BlockSpec(memory_space=pltpu.VMEM)
    return pl.pallas_call(
        kernel,
        out_shape=jax.ShapeDtypeStruct(velocity.shape, f32),
        in_specs=[smem, smem, smem, far, far, far],
        out_specs=vmem,
        scratch_shapes=scratch,
        compiler_params=pltpu.CompilerParams(
            collective_id=0, has_side_effects=True, vmem_limit_bytes=63 * 1024 * 1024
        ),
    )(target, fish, fish_forcing.T, old_adjoint, velocity, chi)


def solution(mesh):
    return jax.shard_map(
        body,
        mesh=mesh,
        in_specs=(
            P(None, ("stream", "span", "depth"), None),
            P(("stream", "span", "depth")),
            P(None, "stream", "span", "depth"),
            P("stream", "span", "depth"),
            P("stream", "span", "depth"),
            P(),
        ),
        out_specs=P(None, "stream", "span", "depth"),
        check_vma=False,
    )
```

```python
import functools

import jax
import jax.numpy as jnp
from jax import lax
from jax.experimental import pallas as pl
from jax.experimental.pallas import tpu as pltpu
from jax.sharding import PartitionSpec as P

SECTIONS = 2
ADVECT = 0.1
DIFFUSE = 0.1
LEVELS = 32767.0

RING = 8
CHIPS = 4
SLOTS = 8
EDGE = 16
PARTS = 6
TILES = 16
LAST = 7
MESH = pl.DeviceIdType.MESH


def lanes_of(shape):
    return lax.broadcasted_iota(jnp.int32, shape, len(shape) - 1)


def rows_of(shape):
    return lax.broadcasted_iota(jnp.int32, shape, len(shape) - 2)


def swap_groups(tiles):
    row, group = rows_of((8, 128)), lanes_of((8, 128)) // EDGE
    for bit in (1, 2, 4):
        row_bit, group_bit = (row & bit) != 0, (group & bit) != 0
        same, moved = row_bit == group_bit, []
        for tile in tiles:
            down = pltpu.roll(pltpu.roll(tile, bit, 0), 128 - EDGE * bit, 1)
            up = down
            if bit != 4:
                up = pltpu.roll(pltpu.roll(tile, 8 - bit, 0), EDGE * bit, 1)
            moved.append(jnp.where(same, tile, jnp.where(row_bit, down, up)))
        tiles = moved
    return tiles


def pack_ends(tiles):
    place = ((lanes_of((8, 128)) + 2) & 127) // 4
    shift = 1
    while len(tiles) > 1:
        later = (place & shift) != 0
        tiles = [
            jnp.where(later, pltpu.roll(b, 4 * shift, 1), a)
            for a, b in zip(tiles[0::2], tiles[1::2])
        ]
        shift *= 2
    return tiles[0]


def advected(here, near, carried, slope):
    values = []
    for c in range(3):
        value = here[c]
        for k in range(3):
            value = value + carried[k] * (near[c][2 * k + 1] - near[c][2 * k])
            value = value - here[k] * slope(c, k)
        values.append(value)
    return values


def kernel(
    target, fish, forcing, old_far, velocity_far, chi_far, out, old, velocity, chi,
    gathered, meta, staged, outgoing, out_scales, incoming, in_scales, decoded,
    found, found_s, fields, face_y, halo_y, face_z, halo_z, corners, corners_in, edge_z,
    moved_x, moved_y, moved_z, slopes, slopes_y, slopes_z, carried_z, weight, pull,
    send_sems, recv_sems, local_sems,
):
    stream, span, depth = (lax.axis_index(a) for a in ("stream", "span", "depth"))
    chip, core = stream // 2, stream % 2
    other_core = {"stream": chip * 2 + 1 - core}

    def along(axis, index, step):
        return {axis: (index + step + RING) % RING}

    copies = {}

    def send(key, src, dst, device):
        number = len(copies)
        copy = pltpu.make_async_remote_copy(
            src_ref=src,
            dst_ref=dst,
            send_sem=send_sems.at[number],
            recv_sem=recv_sems.at[number],
            device_id=device,
            device_id_type=MESH,
        )
        copies[key] = copy
        copy.start()

    fetched = [
        pltpu.make_async_copy(src, dst, local_sems.at[i])
        for i, (src, dst) in enumerate(((old_far, old), (velocity_far, velocity), (chi_far, chi)))
    ]
    for copy in fetched:
        copy.start()

    barrier = pltpu.get_barrier_semaphore()
    partners = [along("span", span, 1), along("span", span, -1)]
    partners += [along("depth", depth, 1), along("depth", depth, -1)]
    partners += [along("stream", stream, s) for s in (1, -1, 2, 4, 6)]
    sides = (-1, 1)
    beside = {"stream": stream, "span": span, "depth": depth}

    def diagonal(axis, step, other, other_step):
        return {**along(axis, beside[axis], step), **along(other, beside[other], other_step)}

    pairs = (("stream", "span"), ("stream", "depth"), ("span", "depth"))
    partners += [diagonal(a, i, b, j) for a, b in pairs for i in sides for j in sides]
    for partner in partners:
        pl.semaphore_signal(barrier, inc=1, device_id=partner, device_id_type=MESH)

    fetched[0].wait()
    tops = [jnp.abs(old[c, :, 0:128]) for c in range(3)]
    for t in range(1, 2 * TILES):
        for c in range(3):
            tops[c] = jnp.maximum(tops[c], jnp.abs(old[c, :, 128 * t : 128 * t + 128]))
    top = jnp.maximum(jnp.maximum(tops[0], tops[1]), tops[2])
    meta[0, 0] = top * (1.0 / LEVELS)
    inverse = LEVELS / jnp.maximum(top, 1e-30)
    for kind in range(PARTS):
        c, first = kind // 2, kind % 2 * TILES
        for t in range(TILES):
            begin = 128 * (first + t)
            staged[kind][pl.ds(t, SLOTS, stride=TILES), :] = jnp.round(old[c, :, begin : begin + 128] * inverse)
        for b in range(SLOTS):
            codes = staged[kind][TILES * b : TILES * (b + 1), :]
            gathered[kind][b] = codes.astype(jnp.int32).astype(jnp.int16)
    label = jnp.zeros((8, 128), jnp.int32)
    for b in range(SLOTS):
        label = jnp.where(rows_of((8, 128)) == b, target[b], label)
    meta[0, 1] = label.astype(jnp.float32)

    pl.semaphore_wait(barrier, len(partners))

    def places(kind, place, count=8, skip=0):
        if kind == PARTS:
            return meta.at[pl.ds(place, count // 8)]
        return gathered[kind].at[pl.ds(8 * place + skip, count)]

    def hop_right(kind, hop):
        source = max(2 * hop - 3, 0)
        count = 4 if hop == 4 and kind < PARTS else 8
        send(("r", kind, hop), places(kind, source, count), places(kind, 2 * hop - 1, count), along("span", span, 1))

    def hop_left(kind, hop):
        source, to, count, skip = 2 * hop - 2, 2 * hop, 8, 0
        if hop == 4:
            to, count, skip = LAST, 4, 4
        send(("l", kind, hop), places(kind, source, count, skip), places(kind, to, count, skip), along("span", span, -1))

    def to_core(kind, hop):
        first = max(2 * hop - 1, 0)
        count = 8 if hop in (0, 4) else 16
        send(("c", kind, hop), places(kind, first, count), places(kind, 8 + first, count), other_core)

    kinds = (PARTS, *range(PARTS))
    for kind in kinds:
        hop_right(kind, 1)
        hop_left(kind, 1)
    for kind in kinds:
        to_core(kind, 0)

    wide, small = (EDGE, 128), (8, 128)
    lane, row, lane8, row8 = lanes_of(wide), rows_of(wide), lanes_of(small), rows_of(small)
    place8 = ((lane8 + 1) & 127) // 4
    after8 = (lane8 & 3) == 3
    odd8 = (place8 & 1) == 1

    def keep_row(n, i, c, y, layer, value):
        face_y[n][y][layer * 3 + c, i : i + 1, :] = value
        if layer == 0 and i in (0, EDGE - 1):
            corners[n][(i > 0) * 2 + y, c : c + 1, :] = value

    def keep_faces(n, i, c, value):
        for layer in (0, 1):
            keep_row(n, i, c, 0, layer, value[layer : layer + 1])
            keep_row(n, i, c, 1, layer, value[EDGE - 1 - layer : EDGE - layer])

    def start_halo(n, tiles):
        field = fields[n]
        for y in (1, 0):
            send((n, "y", y), face_y[n][y], halo_y[n].at[1 - y], along("span", span, sides[y]))
        for c in range(3):
            face_z[n][c] = pack_ends(tiles[c])
        for z in (0, 1):
            send((n, "z", z), face_z[n], halo_z[n].at[1 - z], along("depth", depth, sides[z]))
        send((n, "x", 1), field.at[pl.ds(48, 6)], field.at[pl.ds(0, 6)], along("stream", stream, 1))
        send((n, "x", 0), field.at[pl.ds(6, 6)], field.at[pl.ds(54, 6)], along("stream", stream, -1))
        for x in (0, 1):
            for y in (0, 1):
                send(
                    (n, "xy", x, y),
                    corners[n].at[2 * x + y],
                    corners_in[n].at[3 - 2 * x - y],
                    diagonal("stream", sides[x], "span", sides[y]),
                )
        for number, axis in enumerate(("stream", "span")):
            for i in (0, 1):
                for z in (0, 1):
                    send(
                        (n, axis, i, z),
                        face_z[n],
                        edge_z[n].at[4 * number + 3 - 2 * i - z],
                        diagonal(axis, sides[i], "depth", sides[z]),
                    )

    def ends(before, after, c, layer=1):
        low = jnp.where(depth == 0, 0.0, pltpu.roll(before[c], layer, 1))
        high = jnp.where(depth == RING - 1, 0.0, pltpu.roll(after[c], 128 - layer, 1))
        return jnp.where(after8, high, low)

    def finish_faces(n):
        for axis in ("x", "y", "z"):
            for side in (0, 1):
                copies[(n, axis, side)].wait_recv()
        for end, x in ((0, 0), (RING - 1, 1)):

            @pl.when(stream == end)
            def _():
                fields[n][54 * x : 54 * x + 6] = jnp.zeros((6, EDGE, 128), jnp.float32)

            @pl.when(span == end)
            def _():
                halo_y[n][x] = jnp.zeros((6, EDGE, 128), jnp.float32)

        return [ends(halo_z[n].at[0], halo_z[n].at[1], c) for c in range(3)]

    def finish_diagonals(n):
        for key in [key for key in copies if key[0] == n and key[1] in ("xy", "stream", "span")]:
            copies[key].wait_recv()
        for end, x in ((0, 0), (RING - 1, 1)):

            @pl.when(stream == end)
            def _():
                for y in (0, 1):
                    corners_in[n][2 * x + y] = jnp.zeros(small, jnp.float32)

            @pl.when(span == end)
            def _():
                for y in (0, 1):
                    corners_in[n][2 * y + x] = jnp.zeros(small, jnp.float32)

        second = [ends(halo_z[n].at[0], halo_z[n].at[1], c, 2) for c in range(3)]
        outside = (stream == 0, stream == RING - 1, span == 0, span == RING - 1)
        edges = [
            [
                jnp.where(outside[e], 0.0, ends(edge_z[n].at[2 * e], edge_z[n].at[2 * e + 1], c))
                for c in range(3)
            ]
            for e in range(4)
        ]
        return second, edges

    def around(planes, low, high, ends, first):
        before, here, after = planes
        y_before = jnp.where(row == 0, low, pltpu.roll(here, 1, 0))
        y_after = jnp.where(row == EDGE - 1, high, pltpu.roll(here, EDGE - 1, 0))
        end = jnp.concatenate(
            [pltpu.roll(ends, (128 - 4 * v) % 128, 1) for v in (first, first + 1)], axis=0
        )
        z_before = jnp.where(lane == 0, end, pltpu.roll(here, 1, 1))
        z_after = jnp.where(lane == 127, end, pltpu.roll(here, 127, 1))
        return before, after, y_before, y_after, z_before, z_after

    def plane_near(n, halo, i, c):
        beyond, _, edges = halo
        planes = [fields[n][(i + 1 + d) * 3 + c] for d in range(3)]
        if i < 0:
            low, high = (corners_in[n][y, c : c + 1, :] for y in (0, 1))
            return around(planes, low, high, edges[0][c], 30)
        if i == EDGE:
            low, high = (corners_in[n][2 + y, c : c + 1, :] for y in (0, 1))
            return around(planes, low, high, edges[1][c], 0)
        low, high = (halo_y[n][y, c, i : i + 1, :] for y in (0, 1))
        return around(planes, low, high, beyond[c], 2 * i)

    def row_near(n, halo, y, c):
        here, outer, inner = halo_y[n][y, c], halo_y[n][y, 3 + c], face_y[n][y][c]
        x_before = jnp.where(row == 0, corners_in[n][y, c : c + 1, :], pltpu.roll(here, 1, 0))
        x_after = jnp.where(row == EDGE - 1, corners_in[n][2 + y, c : c + 1, :], pltpu.roll(here, EDGE - 1, 0))
        edge = halo[2][2 + y][c][7 - 7 * y : 8 - 7 * y, :]
        columns = [
            jnp.sum(jnp.where(lane == ((8 * row + 4 - 4 * y - z) & 127), edge, 0.0), axis=1, keepdims=True)
            for z in (0, 1)
        ]
        z_before = jnp.where(lane == 0, columns[0], pltpu.roll(here, 1, 1))
        z_after = jnp.where(lane == 127, columns[1], pltpu.roll(here, 127, 1))
        y_pair = (inner, outer) if y else (outer, inner)
        return x_before, x_after, *y_pair, z_before, z_after

    def end_near(n, halo, c):
        here, outer, inner = halo[0][c], halo[1][c], face_z[n][c]
        x_low, x_high, y_low, y_high = (edge[c] for edge in halo[2])
        x_before = jnp.where(place8 < 2, pltpu.roll(x_low, 8, 1), pltpu.roll(here, 8, 1))
        x_after = jnp.where(place8 >= 30, pltpu.roll(x_high, 120, 1), pltpu.roll(here, 120, 1))
        into = jnp.where(odd8, pltpu.roll(here, 4, 1), pltpu.roll(y_low, 124, 1))
        y_before = jnp.where(row8 == 0, pltpu.roll(into, 1, 0), pltpu.roll(here, 1, 0))
        into = jnp.where(odd8, pltpu.roll(y_high, 4, 1), pltpu.roll(here, 124, 1))
        y_after = jnp.where(row8 == 7, pltpu.roll(into, 7, 0), pltpu.roll(here, 7, 0))
        z_before = jnp.where(after8, inner, outer)
        z_after = jnp.where(after8, outer, inner)
        return x_before, x_after, y_before, y_after, z_before, z_after

    fetched[1].wait()
    tiles = [[], [], []]
    for i in range(EDGE):
        for c in range(3):
            value = velocity[c, i].astype(jnp.float32)
            fields[2][(i + 2) * 3 + c] = value
            keep_faces(2, i, c, value)
            tiles[c] += [value[0:8], value[8:16]]
    start_halo(2, tiles)

    def forward(kind, hop):
        copies[("r", kind, hop)].wait_recv()
        if hop < 4:
            hop_right(kind, hop + 1)
        if hop < 4 or kind < PARTS:
            copies[("l", kind, hop)].wait_recv()
        if hop < 3 or hop == 3 and kind < PARTS:
            hop_left(kind, hop + 1)
        to_core(kind, hop)

    for kind in kinds:
        forward(kind, 1)

    for kind in kinds:
        forward(kind, 2)

    for kind in kinds:
        forward(kind, 3)
    for kind in (PARTS, 0, 1, 2):
        forward(kind, 4)
    for hop in range(5):
        copies[("c", PARTS, hop)].wait_recv()

    owner = (2 * ((chip + lane8 // 8) % CHIPS) + core) * RING + span
    wanted = jnp.where(lane8 < CHIPS * SLOTS, owner * SLOTS + lane8 % 8, -1).astype(jnp.float32)
    at = jnp.zeros(small, jnp.float32)
    for e in range(16):
        at = at + jnp.where(meta[e, 1] == wanted, (row8 + (8 * e + 1)).astype(jnp.float32), 0.0)
    found[...] = jnp.broadcast_to(jnp.sum(at, axis=0, keepdims=True), small).astype(jnp.int32)
    copy = pltpu.make_async_copy(found, found_s, local_sems.at[3])
    copy.start()
    copy.wait()
    where_from = []
    for q in range(CHIPS * SLOTS):
        k, j = q // SLOTS, q % SLOTS
        code = found_s[0, q]
        block = jnp.minimum(jnp.maximum(code - 1, 0), 127)
        where_from.append(block)
        scale = meta[block >> 3, 0, pl.ds(block & 7, 1), :] * jnp.where(code > 0, 1.0, 0.0)
        if k == 0:
            in_scales[0, j : j + 1, :] = scale
        else:
            out_scales[k - 1, j : j + 1, :] = scale
    for k in (2, 1, 3):
        send(("s", k), out_scales.at[k - 1], in_scales.at[k], along("stream", stream, 2 * k))

    def pick(kind):
        for hop in range(5):
            copies[("c", kind, hop)].wait_recv()
        for k in (2, 1, 3, 0):
            for j in range(SLOTS):
                block = gathered[kind][where_from[k * SLOTS + j]]
                if k == 0:
                    incoming[kind][0, j] = block
                else:
                    outgoing[kind][k - 1, j] = block
            if k:
                send(("x", kind, k), outgoing[kind].at[k - 1], incoming[kind].at[k], along("stream", stream, 2 * k))

    for kind in range(PARTS):
        pick(kind)
        if kind + 3 < PARTS:
            forward(kind + 3, 4)

    fetched[2].wait()
    group = lane // EDGE
    forces = []
    for c in range(3):
        force = jnp.zeros(wide, jnp.float32)
        for b in range(SLOTS):
            force = jnp.where(group == b, forcing[c, fish[0, 0, b]], force)
        forces.append(force)
    for i in range(EDGE):
        level = chi[i]
        share = 1.0 / (1.0 + level)
        weight[i] = share
        for c in range(3):
            pull[i * 3 + c] = level * share * forces[c]

    beyond = finish_faces(2)
    halo = (beyond, *finish_diagonals(2))
    for k in range(3):
        carried_z[k] = ADVECT * halo[0][k]
        beside_ends = end_near(2, halo, k)
        beside_rows = [row_near(2, halo, y, k) for y in (0, 1)]
        for axis in range(3):
            slopes_z[axis * 3 + k] = ADVECT * (beside_ends[2 * axis + 1] - beside_ends[2 * axis])
            for y in (0, 1):
                slopes_y[y * 9 + axis * 3 + k] = ADVECT * (beside_rows[y][2 * axis + 1] - beside_rows[y][2 * axis])
    for i in range(-1, EDGE + 1):
        for k in range(3):
            near = plane_near(2, halo, i, k)
            for axis in range(3):
                slopes[(axis * 3 + k) * 18 + i + 1] = ADVECT * (near[2 * axis + 1] - near[2 * axis])


    for k in (2, 1, 3):
        copies[("s", k)].wait_recv()
    tiles = [[], [], []]
    for kind in range(PARTS):
        c, first = kind // 2, kind % 2 * (EDGE // 2)
        for k in (2, 1, 3):
            copies[("x", kind, k)].wait_recv()
        for j in range(SLOTS):
            total = incoming[kind][0, j].astype(jnp.float32) * in_scales[0, j : j + 1, :]
            for k in range(1, CHIPS):
                total = total + incoming[kind][k, j].astype(jnp.float32) * in_scales[k, j : j + 1, :]
            decoded[kind][TILES * j : TILES * (j + 1), :] = total
        moved = swap_groups([decoded[kind][pl.ds(t, SLOTS, stride=TILES), :] for t in range(TILES)])
        tiles[c] += moved
        for t, tile in enumerate(moved):
            i, h = first + t // 2, t % 2
            fields[0][(i + 2) * 3 + c, 8 * h : 8 * h + 8, :] = tile
            for layer in (0, 1):
                at = 7 - layer if h else layer
                keep_row(0, i, c, h, layer, tile[at : at + 1])

    for section in range(SECTIONS):
        start_halo(section, tiles)
        beyond = finish_faces(section)
        halo = (beyond, None, None)
        for i in (*range(EDGE), -1, EDGE):
            if i < 0:
                halo = (beyond, *finish_diagonals(section))
            here = [fields[section][(i + 2) * 3 + c] for c in range(3)]
            near = [plane_near(section, halo, i, c) for c in range(3)]
            carried = [ADVECT * fields[2][(i + 2) * 3 + k] for k in range(3)]
            values = advected(here, near, carried, lambda c, k: slopes[(c * 3 + k) * 18 + i + 1])
            for c in range(3):
                value = values[c]
                if i in (-1, EDGE):
                    value = jnp.where(stream == (0 if i < 0 else RING - 1), 0.0, value)
                moved_x[(i + 1) * 3 + c] = value
        here = beyond
        near = [end_near(section, halo, c) for c in range(3)]
        values = advected(here, near, [carried_z[k] for k in range(3)], lambda c, k: slopes_z[c * 3 + k])
        for c in range(3):
            moved_z[c] = jnp.where(jnp.where(after8, RING - 1, 0) == depth, 0.0, values[c])
        for y in (0, 1):
            here = [halo_y[section][y, c] for c in range(3)]
            near = [row_near(section, halo, y, c) for c in range(3)]
            carried = [ADVECT * halo_y[2][y, k] for k in range(3)]
            values = advected(here, near, carried, lambda c, k: slopes_y[y * 9 + c * 3 + k])
            for c in range(3):
                moved_y[y * 3 + c] = jnp.where(span == (RING - 1) * y, 0.0, values[c])
        tiles = [[], [], []]
        for i in range(EDGE):
            share = weight[i]
            for c in range(3):
                planes = [moved_x[(i + d) * 3 + c] for d in range(3)]
                low, high = (moved_y[y * 3 + c, i : i + 1, :] for y in (0, 1))
                near = around(planes, low, high, moved_z[c], 2 * i)
                total = (near[0] + near[1]) + (near[2] + near[3]) + (near[4] + near[5])
                value = (planes[1] + DIFFUSE * (total - 6.0 * planes[1])) * share + pull[i * 3 + c]
                if section == SECTIONS - 1:
                    out[c, i] = value
                else:
                    fields[section + 1][(i + 2) * 3 + c] = value
                    keep_faces(section + 1, i, c, value)
                    tiles[c] += [value[0:8], value[8:16]]

    for copy in copies.values():
        copy.wait_send()


def body(old_adjoint, target, velocity, chi, fish, fish_forcing):
    f32, i16 = jnp.float32, jnp.int16
    v = pltpu.VMEM
    scratch = [
        v((3, SLOTS, 2 * TILES * 128), f32),
        v(velocity.shape, velocity.dtype),
        v(chi.shape, f32),
        [v((128, TILES, 128), i16)] * PARTS,
        v((16, 2, 8, 128), f32),
        [v((SLOTS * TILES, 128), f32)] * PARTS,
        [v((CHIPS - 1, SLOTS, TILES, 128), i16)] * PARTS,
        v((CHIPS - 1, SLOTS, 128), f32),
        [v((CHIPS, SLOTS, TILES, 128), i16)] * PARTS,
        v((CHIPS, SLOTS, 128), f32),
        [v((SLOTS * TILES, 128), f32)] * PARTS,
        v((8, 128), jnp.int32),
        pltpu.SMEM((8, 128), jnp.int32),
        [v((20 * 3, EDGE, 128), f32)] * 3,
        [[v((6, EDGE, 128), f32)] * 2] * 3,
        [v((2, 6, EDGE, 128), f32)] * 3,
        [v((3, 8, 128), f32)] * 3,
        [v((2, 3, 8, 128), f32)] * 3,
        [v((4, 8, 128), f32)] * 3,
        [v((4, 8, 128), f32)] * 3,
        [v((8, 3, 8, 128), f32)] * 3,
        v((18 * 3, EDGE, 128), f32),
        v((6, EDGE, 128), f32),
        v((3, 8, 128), f32),
        v((9 * 18, EDGE, 128), f32),
        v((18, EDGE, 128), f32),
        v((9, 8, 128), f32),
        v((3, 8, 128), f32),
        v((EDGE, EDGE, 128), f32),
        v((3 * EDGE, EDGE, 128), f32),
        pltpu.SemaphoreType.DMA((192,)),
        pltpu.SemaphoreType.DMA((192,)),
        pltpu.SemaphoreType.DMA((4,)),
    ]
    smem = pl.BlockSpec(memory_space=pltpu.SMEM)
    far = pl.BlockSpec(memory_space=pl.ANY)
    vmem = pl.BlockSpec(memory_space=pltpu.VMEM)
    return pl.pallas_call(
        kernel,
        out_shape=jax.ShapeDtypeStruct(velocity.shape, f32),
        in_specs=[smem, smem, smem, far, far, far],
        out_specs=vmem,
        scratch_shapes=scratch,
        compiler_params=pltpu.CompilerParams(
            collective_id=0, has_side_effects=True, vmem_limit_bytes=63 * 1024 * 1024
        ),
    )(target, fish, fish_forcing.T, old_adjoint, velocity, chi)


def solution(mesh):
    return jax.shard_map(
        body,
        mesh=mesh,
        in_specs=(
            P(None, ("stream", "span", "depth"), None),
            P(("stream", "span", "depth")),
            P(None, "stream", "span", "depth"),
            P("stream", "span", "depth"),
            P("stream", "span", "depth"),
            P(),
        ),
        out_specs=P(None, "stream", "span", "depth"),
        check_vma=False,
    )
```

```python
import functools

import jax
import jax.numpy as jnp
from jax import lax
from jax.experimental import pallas as pl
from jax.experimental.pallas import tpu as pltpu
from jax.sharding import PartitionSpec as P

SECTIONS = 2
ADVECT = 0.1
DIFFUSE = 0.1
LEVELS = 32767.0

RING = 8
CHIPS = 4
SLOTS = 8
EDGE = 16
PARTS = 3
EACH = PARTS // 3
TILES = 32 // EACH
LAST = 7
MESH = pl.DeviceIdType.MESH


def lanes_of(shape):
    return lax.broadcasted_iota(jnp.int32, shape, len(shape) - 1)


def rows_of(shape):
    return lax.broadcasted_iota(jnp.int32, shape, len(shape) - 2)


def swap_groups(tiles):
    row, group = rows_of((8, 128)), lanes_of((8, 128)) // EDGE
    for bit in (1, 2, 4):
        row_bit, group_bit = (row & bit) != 0, (group & bit) != 0
        same, moved = row_bit == group_bit, []
        for tile in tiles:
            down = pltpu.roll(pltpu.roll(tile, bit, 0), 128 - EDGE * bit, 1)
            up = down
            if bit != 4:
                up = pltpu.roll(pltpu.roll(tile, 8 - bit, 0), EDGE * bit, 1)
            moved.append(jnp.where(same, tile, jnp.where(row_bit, down, up)))
        tiles = moved
    return tiles


def pack_ends(tiles):
    place = ((lanes_of((8, 128)) + 2) & 127) // 4
    shift = 1
    while len(tiles) > 1:
        later = (place & shift) != 0
        tiles = [
            jnp.where(later, pltpu.roll(b, 4 * shift, 1), a)
            for a, b in zip(tiles[0::2], tiles[1::2])
        ]
        shift *= 2
    return tiles[0]


def advected(here, near, carried, slope):
    values = []
    for c in range(3):
        value = here[c]
        for k in range(3):
            value = value + carried[k] * (near[c][2 * k + 1] - near[c][2 * k])
            value = value - here[k] * slope(c, k)
        values.append(value)
    return values


def kernel(
    target, fish, forcing, old_far, velocity_far, chi_far, out, old, velocity, chi,
    gathered, meta, staged, outgoing, out_scales, incoming, in_scales, decoded,
    found, found_s, fields, face_y, halo_y, face_z, halo_z, corners, corners_in, edge_z,
    moved_x, moved_y, moved_z, slopes, slopes_y, slopes_z, carried_z, weight, pull,
    send_sems, recv_sems, local_sems,
):
    stream, span, depth = (lax.axis_index(a) for a in ("stream", "span", "depth"))
    chip, core = stream // 2, stream % 2
    other_core = {"stream": chip * 2 + 1 - core}

    def along(axis, index, step):
        return {axis: (index + step + RING) % RING}

    copies = {}

    def send(key, src, dst, device):
        number = len(copies)
        copy = pltpu.make_async_remote_copy(
            src_ref=src,
            dst_ref=dst,
            send_sem=send_sems.at[number],
            recv_sem=recv_sems.at[number],
            device_id=device,
            device_id_type=MESH,
        )
        copies[key] = copy
        copy.start()

    fetched = [
        pltpu.make_async_copy(src, dst, local_sems.at[i])
        for i, (src, dst) in enumerate(((old_far, old), (velocity_far, velocity), (chi_far, chi)))
    ]
    for copy in fetched:
        copy.start()

    barrier = pltpu.get_barrier_semaphore()
    partners = [along("span", span, 1), along("span", span, -1)]
    partners += [along("depth", depth, 1), along("depth", depth, -1)]
    partners += [along("stream", stream, s) for s in (1, -1, 2, 4, 6)]
    sides = (-1, 1)
    beside = {"stream": stream, "span": span, "depth": depth}

    def diagonal(axis, step, other, other_step):
        return {**along(axis, beside[axis], step), **along(other, beside[other], other_step)}

    for partner in partners:
        pl.semaphore_signal(barrier, inc=1, device_id=partner, device_id_type=MESH)

    fetched[0].wait()
    tops = [jnp.abs(old[c, :, 0:128]) for c in range(3)]
    for t in range(1, EACH * TILES):
        for c in range(3):
            tops[c] = jnp.maximum(tops[c], jnp.abs(old[c, :, 128 * t : 128 * t + 128]))
    top = jnp.maximum(jnp.maximum(tops[0], tops[1]), tops[2])
    meta[0, 0] = top * (1.0 / LEVELS)
    inverse = LEVELS / jnp.maximum(top, 1e-30)
    for kind in range(PARTS):
        c, first = kind // EACH, kind % EACH * TILES
        for t in range(TILES):
            begin = 128 * (first + t)
            staged[kind][pl.ds(t, SLOTS, stride=TILES), :] = jnp.round(old[c, :, begin : begin + 128] * inverse)
        for b in range(SLOTS):
            codes = staged[kind][TILES * b : TILES * (b + 1), :]
            gathered[kind][b] = codes.astype(jnp.int32).astype(jnp.int16)
    label = jnp.zeros((8, 128), jnp.int32)
    for b in range(SLOTS):
        label = jnp.where(rows_of((8, 128)) == b, target[b], label)
    meta[0, 1] = label.astype(jnp.float32)

    pl.semaphore_wait(barrier, len(partners))

    def places(kind, place, count=8, skip=0):
        if kind == PARTS:
            return meta.at[pl.ds(place, count // 8)]
        return gathered[kind].at[pl.ds(8 * place + skip, count)]

    def hop_right(kind, hop):
        source = max(2 * hop - 3, 0)
        count = 4 if hop == 4 and kind < PARTS else 8
        send(("r", kind, hop), places(kind, source, count), places(kind, 2 * hop - 1, count), along("span", span, 1))

    def hop_left(kind, hop):
        source, to, count, skip = 2 * hop - 2, 2 * hop, 8, 0
        if hop == 4:
            to, count, skip = LAST, 4, 4
        send(("l", kind, hop), places(kind, source, count, skip), places(kind, to, count, skip), along("span", span, -1))

    def to_core(kind, hop):
        first = max(2 * hop - 1, 0)
        count = 8 if hop in (0, 4) else 16
        send(("c", kind, hop), places(kind, first, count), places(kind, 8 + first, count), other_core)

    kinds = (PARTS, *range(PARTS))
    for kind in kinds:
        hop_right(kind, 1)
        hop_left(kind, 1)
    for kind in kinds:
        to_core(kind, 0)

    wide, small = (EDGE, 128), (8, 128)
    lane, row, lane8, row8 = lanes_of(wide), rows_of(wide), lanes_of(small), rows_of(small)
    place8 = ((lane8 + 1) & 127) // 4
    after8 = (lane8 & 3) == 3
    odd8 = (place8 & 1) == 1

    def keep_row(n, i, c, y, layer, value):
        face_y[n][y][layer * 3 + c, i : i + 1, :] = value
        if layer == 0 and i in (0, EDGE - 1):
            corners[n][(i > 0) * 2 + y, c : c + 1, :] = value

    def keep_faces(n, i, c, value):
        for layer in (0, 1):
            keep_row(n, i, c, 0, layer, value[layer : layer + 1])
            keep_row(n, i, c, 1, layer, value[EDGE - 1 - layer : EDGE - layer])

    def start_faces(n, tiles):
        field = fields[n]
        for y in (1, 0):
            send(
                (n, "y", y),
                face_y[n][y].at[pl.ds(0, 3)],
                halo_y[n].at[1 - y, pl.ds(0, 3)],
                along("span", span, sides[y]),
            )
        for c in range(3):
            face_z[n][c] = pack_ends(tiles[c])
        for z in (0, 1):
            send((n, "z", z), face_z[n], halo_z[n].at[1 - z], along("depth", depth, sides[z]))
        send((n, "x", 1), field.at[pl.ds(51, 3)], field.at[pl.ds(3, 3)], along("stream", stream, 1))
        send((n, "x", 0), field.at[pl.ds(6, 3)], field.at[pl.ds(54, 3)], along("stream", stream, -1))

    def start_diagonals(n):
        field = fields[n]
        for x in (0, 1):
            for y in (0, 1):
                send(
                    (n, "xy", x, y),
                    corners[n].at[2 * x + y],
                    corners_in[n].at[3 - 2 * x - y],
                    diagonal("stream", sides[x], "span", sides[y]),
                )
        for number, axis in enumerate(("stream", "span")):
            for i in (0, 1):
                for z in (0, 1):
                    send(
                        (n, axis, i, z),
                        face_z[n],
                        edge_z[n].at[4 * number + 3 - 2 * i - z],
                        diagonal(axis, sides[i], "depth", sides[z]),
                    )
        for y in (1, 0):
            send(
                (n, "y2", y),
                face_y[n][y].at[pl.ds(3, 3)],
                halo_y[n].at[1 - y, pl.ds(3, 3)],
                along("span", span, sides[y]),
            )
        send((n, "x2", 1), field.at[pl.ds(48, 3)], field.at[pl.ds(0, 3)], along("stream", stream, 1))
        send((n, "x2", 0), field.at[pl.ds(9, 3)], field.at[pl.ds(57, 3)], along("stream", stream, -1))

    def ends(before, after, c, layer=1):
        low = jnp.where(depth == 0, 0.0, pltpu.roll(before[c], layer, 1))
        high = jnp.where(depth == RING - 1, 0.0, pltpu.roll(after[c], 128 - layer, 1))
        return jnp.where(after8, high, low)

    def finish_faces(n):
        for axis in ("x", "y", "z"):
            for side in (0, 1):
                copies[(n, axis, side)].wait_recv()
        for end, x in ((0, 0), (RING - 1, 1)):

            @pl.when(stream == end)
            def _():
                fields[n][3 + 51 * x : 6 + 51 * x] = jnp.zeros((3, EDGE, 128), jnp.float32)

            @pl.when(span == end)
            def _():
                halo_y[n][x, 0:3] = jnp.zeros((3, EDGE, 128), jnp.float32)

        return [ends(halo_z[n].at[0], halo_z[n].at[1], c) for c in range(3)]

    def finish_diagonals(n):
        for key in [key for key in copies if key[0] == n and key[1] not in ("x", "y", "z")]:
            copies[key].wait_recv()
        for end, x in ((0, 0), (RING - 1, 1)):

            @pl.when(stream == end)
            def _():
                fields[n][57 * x : 57 * x + 3] = jnp.zeros((3, EDGE, 128), jnp.float32)
                for y in (0, 1):
                    corners_in[n][2 * x + y] = jnp.zeros(small, jnp.float32)

            @pl.when(span == end)
            def _():
                halo_y[n][x, 3:6] = jnp.zeros((3, EDGE, 128), jnp.float32)
                for y in (0, 1):
                    corners_in[n][2 * y + x] = jnp.zeros(small, jnp.float32)

        second = [ends(halo_z[n].at[0], halo_z[n].at[1], c, 2) for c in range(3)]
        outside = (stream == 0, stream == RING - 1, span == 0, span == RING - 1)
        edges = [
            [
                jnp.where(outside[e], 0.0, ends(edge_z[n].at[2 * e], edge_z[n].at[2 * e + 1], c))
                for c in range(3)
            ]
            for e in range(4)
        ]
        return second, edges

    def around(planes, low, high, ends, first):
        before, here, after = planes
        y_before = jnp.where(row == 0, low, pltpu.roll(here, 1, 0))
        y_after = jnp.where(row == EDGE - 1, high, pltpu.roll(here, EDGE - 1, 0))
        end = jnp.concatenate(
            [pltpu.roll(ends, (128 - 4 * v) % 128, 1) for v in (first, first + 1)], axis=0
        )
        z_before = jnp.where(lane == 0, end, pltpu.roll(here, 1, 1))
        z_after = jnp.where(lane == 127, end, pltpu.roll(here, 127, 1))
        return before, after, y_before, y_after, z_before, z_after

    def plane_near(n, halo, i, c):
        beyond, _, edges = halo
        planes = [fields[n][(i + 1 + d) * 3 + c] for d in range(3)]
        if i < 0:
            low, high = (corners_in[n][y, c : c + 1, :] for y in (0, 1))
            return around(planes, low, high, edges[0][c], 30)
        if i == EDGE:
            low, high = (corners_in[n][2 + y, c : c + 1, :] for y in (0, 1))
            return around(planes, low, high, edges[1][c], 0)
        low, high = (halo_y[n][y, c, i : i + 1, :] for y in (0, 1))
        return around(planes, low, high, beyond[c], 2 * i)

    def row_near(n, halo, y, c):
        here, outer, inner = halo_y[n][y, c], halo_y[n][y, 3 + c], face_y[n][y][c]
        x_before = jnp.where(row == 0, corners_in[n][y, c : c + 1, :], pltpu.roll(here, 1, 0))
        x_after = jnp.where(row == EDGE - 1, corners_in[n][2 + y, c : c + 1, :], pltpu.roll(here, EDGE - 1, 0))
        edge = halo[2][2 + y][c][7 - 7 * y : 8 - 7 * y, :]
        columns = [
            jnp.sum(jnp.where(lane == ((8 * row + 4 - 4 * y - z) & 127), edge, 0.0), axis=1, keepdims=True)
            for z in (0, 1)
        ]
        z_before = jnp.where(lane == 0, columns[0], pltpu.roll(here, 1, 1))
        z_after = jnp.where(lane == 127, columns[1], pltpu.roll(here, 127, 1))
        y_pair = (inner, outer) if y else (outer, inner)
        return x_before, x_after, *y_pair, z_before, z_after

    def end_near(n, halo, c):
        here, outer, inner = halo[0][c], halo[1][c], face_z[n][c]
        x_low, x_high, y_low, y_high = (edge[c] for edge in halo[2])
        x_before = jnp.where(place8 < 2, pltpu.roll(x_low, 8, 1), pltpu.roll(here, 8, 1))
        x_after = jnp.where(place8 >= 30, pltpu.roll(x_high, 120, 1), pltpu.roll(here, 120, 1))
        into = jnp.where(odd8, pltpu.roll(here, 4, 1), pltpu.roll(y_low, 124, 1))
        y_before = jnp.where(row8 == 0, pltpu.roll(into, 1, 0), pltpu.roll(here, 1, 0))
        into = jnp.where(odd8, pltpu.roll(y_high, 4, 1), pltpu.roll(here, 124, 1))
        y_after = jnp.where(row8 == 7, pltpu.roll(into, 7, 0), pltpu.roll(here, 7, 0))
        z_before = jnp.where(after8, inner, outer)
        z_after = jnp.where(after8, outer, inner)
        return x_before, x_after, y_before, y_after, z_before, z_after

    fetched[1].wait()
    tiles = [[], [], []]
    for i in range(EDGE):
        for c in range(3):
            value = velocity[c, i].astype(jnp.float32)
            fields[2][(i + 2) * 3 + c] = value
            keep_faces(2, i, c, value)
            tiles[c] += [value[0:8], value[8:16]]
    start_faces(2, tiles)

    def forward(kind, hop):
        copies[("r", kind, hop)].wait_recv()
        if hop < 4:
            hop_right(kind, hop + 1)
        if hop < 4 or kind < PARTS:
            copies[("l", kind, hop)].wait_recv()
        if hop < 3 or hop == 3 and kind < PARTS:
            hop_left(kind, hop + 1)
        to_core(kind, hop)

    for kind in kinds:
        forward(kind, 1)

    for kind in kinds:
        forward(kind, 2)
    beyond = finish_faces(2)
    start_diagonals(2)

    for kind in kinds:
        forward(kind, 3)
    for kind in (PARTS, *range(PARTS // 2)):
        forward(kind, 4)
    for hop in range(5):
        copies[("c", PARTS, hop)].wait_recv()

    owner = (2 * ((chip + lane8 // 8) % CHIPS) + core) * RING + span
    wanted = jnp.where(lane8 < CHIPS * SLOTS, owner * SLOTS + lane8 % 8, -1).astype(jnp.float32)
    at = jnp.zeros(small, jnp.float32)
    for e in range(16):
        at = at + jnp.where(meta[e, 1] == wanted, (row8 + (8 * e + 1)).astype(jnp.float32), 0.0)
    found[...] = jnp.broadcast_to(jnp.sum(at, axis=0, keepdims=True), small).astype(jnp.int32)
    copy = pltpu.make_async_copy(found, found_s, local_sems.at[3])
    copy.start()
    copy.wait()
    where_from = []
    for q in range(CHIPS * SLOTS):
        k, j = q // SLOTS, q % SLOTS
        code = found_s[0, q]
        block = jnp.minimum(jnp.maximum(code - 1, 0), 127)
        where_from.append(block)
        scale = meta[block >> 3, 0, pl.ds(block & 7, 1), :] * jnp.where(code > 0, 1.0, 0.0)
        if k == 0:
            in_scales[0, j : j + 1, :] = scale
        else:
            out_scales[k - 1, j : j + 1, :] = scale
    for k in (2, 1, 3):
        send(("s", k), out_scales.at[k - 1], in_scales.at[k], along("stream", stream, 2 * k))

    def pick(kind):
        for hop in range(5):
            copies[("c", kind, hop)].wait_recv()
        for k in (2, 1, 3, 0):
            for j in range(SLOTS):
                block = gathered[kind][where_from[k * SLOTS + j]]
                if k == 0:
                    incoming[kind][0, j] = block
                else:
                    outgoing[kind][k - 1, j] = block
            if k:
                send(("x", kind, k), outgoing[kind].at[k - 1], incoming[kind].at[k], along("stream", stream, 2 * k))

    for kind in range(PARTS):
        pick(kind)
        for later in range(PARTS // 2, PARTS) if kind == 0 else ():
            forward(later, 4)

    fetched[2].wait()
    group = lane // EDGE
    forces = []
    for c in range(3):
        force = jnp.zeros(wide, jnp.float32)
        for b in range(SLOTS):
            force = jnp.where(group == b, forcing[c, fish[0, 0, b]], force)
        forces.append(force)
    for i in range(EDGE):
        level = chi[i]
        share = 1.0 / (1.0 + level)
        weight[i] = share
        for c in range(3):
            pull[i * 3 + c] = level * share * forces[c]

    halo = (beyond, *finish_diagonals(2))
    for k in range(3):
        carried_z[k] = ADVECT * halo[0][k]
        beside_ends = end_near(2, halo, k)
        beside_rows = [row_near(2, halo, y, k) for y in (0, 1)]
        for axis in range(3):
            slopes_z[axis * 3 + k] = ADVECT * (beside_ends[2 * axis + 1] - beside_ends[2 * axis])
            for y in (0, 1):
                slopes_y[y * 9 + axis * 3 + k] = ADVECT * (beside_rows[y][2 * axis + 1] - beside_rows[y][2 * axis])
    for i in range(-1, EDGE + 1):
        for k in range(3):
            near = plane_near(2, halo, i, k)
            for axis in range(3):
                slopes[(axis * 3 + k) * 18 + i + 1] = ADVECT * (near[2 * axis + 1] - near[2 * axis])


    for k in (2, 1, 3):
        copies[("s", k)].wait_recv()
    tiles = [[], [], []]
    for kind in range(PARTS):
        c, first = kind // EACH, kind % EACH * (EDGE // EACH)
        for k in (2, 1, 3):
            copies[("x", kind, k)].wait_recv()
        for j in range(SLOTS):
            total = incoming[kind][0, j].astype(jnp.float32) * in_scales[0, j : j + 1, :]
            for k in range(1, CHIPS):
                total = total + incoming[kind][k, j].astype(jnp.float32) * in_scales[k, j : j + 1, :]
            decoded[kind][TILES * j : TILES * (j + 1), :] = total
        moved = swap_groups([decoded[kind][pl.ds(t, SLOTS, stride=TILES), :] for t in range(TILES)])
        tiles[c] += moved
        for t, tile in enumerate(moved):
            i, h = first + t // 2, t % 2
            fields[0][(i + 2) * 3 + c, 8 * h : 8 * h + 8, :] = tile
            for layer in (0, 1):
                at = 7 - layer if h else layer
                keep_row(0, i, c, h, layer, tile[at : at + 1])

    settled = set()
    for section in range(SECTIONS):
        sent = [copy for key, copy in copies.items() if key not in settled]
        settled.update(copies)
        start_faces(section, tiles)
        start_diagonals(section)
        for copy in sent:
            copy.wait_send()
        beyond = finish_faces(section)
        halo = (beyond, None, None)
        for i in (*range(EDGE), -1, EDGE):
            if i < 0:
                halo = (beyond, *finish_diagonals(section))
            here = [fields[section][(i + 2) * 3 + c] for c in range(3)]
            near = [plane_near(section, halo, i, c) for c in range(3)]
            carried = [ADVECT * fields[2][(i + 2) * 3 + k] for k in range(3)]
            values = advected(here, near, carried, lambda c, k: slopes[(c * 3 + k) * 18 + i + 1])
            for c in range(3):
                value = values[c]
                if i in (-1, EDGE):
                    value = jnp.where(stream == (0 if i < 0 else RING - 1), 0.0, value)
                moved_x[(i + 1) * 3 + c] = value
        here = beyond
        near = [end_near(section, halo, c) for c in range(3)]
        values = advected(here, near, [carried_z[k] for k in range(3)], lambda c, k: slopes_z[c * 3 + k])
        for c in range(3):
            moved_z[c] = jnp.where(jnp.where(after8, RING - 1, 0) == depth, 0.0, values[c])
        for y in (0, 1):
            here = [halo_y[section][y, c] for c in range(3)]
            near = [row_near(section, halo, y, c) for c in range(3)]
            carried = [ADVECT * halo_y[2][y, k] for k in range(3)]
            values = advected(here, near, carried, lambda c, k: slopes_y[y * 9 + c * 3 + k])
            for c in range(3):
                moved_y[y * 3 + c] = jnp.where(span == (RING - 1) * y, 0.0, values[c])
        tiles = [[], [], []]
        for i in range(EDGE):
            share = weight[i]
            for c in range(3):
                planes = [moved_x[(i + d) * 3 + c] for d in range(3)]
                low, high = (moved_y[y * 3 + c, i : i + 1, :] for y in (0, 1))
                near = around(planes, low, high, moved_z[c], 2 * i)
                total = (near[0] + near[1]) + (near[2] + near[3]) + (near[4] + near[5])
                value = (planes[1] + DIFFUSE * (total - 6.0 * planes[1])) * share + pull[i * 3 + c]
                if section == SECTIONS - 1:
                    out[c, i] = value
                else:
                    fields[section + 1][(i + 2) * 3 + c] = value
                    keep_faces(section + 1, i, c, value)
                    tiles[c] += [value[0:8], value[8:16]]

    for key, copy in copies.items():
        if key not in settled:
            copy.wait_send()


def body(old_adjoint, target, velocity, chi, fish, fish_forcing):
    f32, i16 = jnp.float32, jnp.int16
    v = pltpu.VMEM
    scratch = [
        v((3, SLOTS, EACH * TILES * 128), f32),
        v(velocity.shape, velocity.dtype),
        v(chi.shape, f32),
        [v((128, TILES, 128), i16)] * PARTS,
        v((16, 2, 8, 128), f32),
        [v((SLOTS * TILES, 128), f32)] * PARTS,
        [v((CHIPS - 1, SLOTS, TILES, 128), i16)] * PARTS,
        v((CHIPS - 1, SLOTS, 128), f32),
        [v((CHIPS, SLOTS, TILES, 128), i16)] * PARTS,
        v((CHIPS, SLOTS, 128), f32),
        [v((SLOTS * TILES, 128), f32)] * PARTS,
        v((8, 128), jnp.int32),
        pltpu.SMEM((8, 128), jnp.int32),
        [v((20 * 3, EDGE, 128), f32)] * 3,
        [[v((6, EDGE, 128), f32)] * 2] * 3,
        [v((2, 6, EDGE, 128), f32)] * 3,
        [v((3, 8, 128), f32)] * 3,
        [v((2, 3, 8, 128), f32)] * 3,
        [v((4, 8, 128), f32)] * 3,
        [v((4, 8, 128), f32)] * 3,
        [v((8, 3, 8, 128), f32)] * 3,
        v((18 * 3, EDGE, 128), f32),
        v((6, EDGE, 128), f32),
        v((3, 8, 128), f32),
        v((9 * 18, EDGE, 128), f32),
        v((18, EDGE, 128), f32),
        v((9, 8, 128), f32),
        v((3, 8, 128), f32),
        v((EDGE, EDGE, 128), f32),
        v((3 * EDGE, EDGE, 128), f32),
        pltpu.SemaphoreType.DMA((192,)),
        pltpu.SemaphoreType.DMA((192,)),
        pltpu.SemaphoreType.DMA((4,)),
    ]
    smem = pl.BlockSpec(memory_space=pltpu.SMEM)
    far = pl.BlockSpec(memory_space=pl.ANY)
    vmem = pl.BlockSpec(memory_space=pltpu.VMEM)
    return pl.pallas_call(
        kernel,
        out_shape=jax.ShapeDtypeStruct(velocity.shape, f32),
        in_specs=[smem, smem, smem, far, far, far],
        out_specs=vmem,
        scratch_shapes=scratch,
        compiler_params=pltpu.CompilerParams(
            collective_id=0, has_side_effects=True, vmem_limit_bytes=63 * 1024 * 1024
        ),
    )(target, fish, fish_forcing.T, old_adjoint, velocity, chi)


def solution(mesh):
    return jax.shard_map(
        body,
        mesh=mesh,
        in_specs=(
            P(None, ("stream", "span", "depth"), None),
            P(("stream", "span", "depth")),
            P(None, "stream", "span", "depth"),
            P("stream", "span", "depth"),
            P("stream", "span", "depth"),
            P(),
        ),
        out_specs=P(None, "stream", "span", "depth"),
        check_vma=False,
    )
```

```python
import functools

import jax
import jax.numpy as jnp
from jax import lax
from jax.experimental import pallas as pl
from jax.experimental.pallas import tpu as pltpu
from jax.sharding import PartitionSpec as P

SECTIONS = 2
ADVECT = 0.1
DIFFUSE = 0.1
LEVELS = 32767.0

RING = 8
CHIPS = 4
SLOTS = 8
EDGE = 16
PARTS = 3
EACH = PARTS // 3
TILES = 32 // EACH
LAST = 7
MESH = pl.DeviceIdType.MESH


def lanes_of(shape):
    return lax.broadcasted_iota(jnp.int32, shape, len(shape) - 1)


def rows_of(shape):
    return lax.broadcasted_iota(jnp.int32, shape, len(shape) - 2)


def swap_groups(tiles):
    row, group = rows_of((8, 128)), lanes_of((8, 128)) // EDGE
    for bit in (1, 2, 4):
        row_bit, group_bit = (row & bit) != 0, (group & bit) != 0
        same, moved = row_bit == group_bit, []
        for tile in tiles:
            down = pltpu.roll(pltpu.roll(tile, bit, 0), 128 - EDGE * bit, 1)
            up = down
            if bit != 4:
                up = pltpu.roll(pltpu.roll(tile, 8 - bit, 0), EDGE * bit, 1)
            moved.append(jnp.where(same, tile, jnp.where(row_bit, down, up)))
        tiles = moved
    return tiles


def pack_ends(tiles):
    place = ((lanes_of((8, 128)) + 2) & 127) // 4
    shift = 1
    while len(tiles) > 1:
        later = (place & shift) != 0
        tiles = [
            jnp.where(later, pltpu.roll(b, 4 * shift, 1), a)
            for a, b in zip(tiles[0::2], tiles[1::2])
        ]
        shift *= 2
    return tiles[0]


def advected(here, near, carried, slope):
    values = []
    for c in range(3):
        value = here[c]
        for k in range(3):
            value = value + carried[k] * (near[c][2 * k + 1] - near[c][2 * k])
            value = value - here[k] * slope(c, k)
        values.append(value)
    return values


def kernel(
    target, fish, forcing, old_far, velocity_far, chi_far, out, old, velocity, chi,
    gathered, meta, staged, outgoing, out_scales, incoming, in_scales, decoded,
    found, found_s, fields, face_y, halo_y, face_z, halo_z, corners, corners_in, edge_z,
    moved_x, moved_y, moved_z, slopes, slopes_y, slopes_z, carried_z, weight, pull,
    send_sems, recv_sems, local_sems,
):
    stream, span, depth = (lax.axis_index(a) for a in ("stream", "span", "depth"))
    chip, core = stream // 2, stream % 2
    other_core = {"stream": chip * 2 + 1 - core}

    def along(axis, index, step):
        return {axis: (index + step + RING) % RING}

    copies = {}

    def send(key, src, dst, device):
        number = len(copies)
        copy = pltpu.make_async_remote_copy(
            src_ref=src,
            dst_ref=dst,
            send_sem=send_sems.at[number],
            recv_sem=recv_sems.at[number],
            device_id=device,
            device_id_type=MESH,
        )
        copies[key] = copy
        copy.start()

    fetched = [
        pltpu.make_async_copy(src, dst, local_sems.at[i])
        for i, (src, dst) in enumerate(((old_far, old), (velocity_far, velocity), (chi_far, chi)))
    ]
    for copy in fetched:
        copy.start()

    barrier = pltpu.get_barrier_semaphore()
    partners = [along("span", span, 1), along("span", span, -1)]
    partners += [along("depth", depth, 1), along("depth", depth, -1)]
    partners += [along("stream", stream, s) for s in (1, -1, 2, 4, 6)]
    sides = (-1, 1)
    beside = {"stream": stream, "span": span, "depth": depth}

    def diagonal(axis, step, other, other_step):
        return {**along(axis, beside[axis], step), **along(other, beside[other], other_step)}

    for partner in partners:
        pl.semaphore_signal(barrier, inc=1, device_id=partner, device_id_type=MESH)

    fetched[0].wait()
    tops = [jnp.abs(old[c, :, 0:128]) for c in range(3)]
    for t in range(1, EACH * TILES):
        for c in range(3):
            tops[c] = jnp.maximum(tops[c], jnp.abs(old[c, :, 128 * t : 128 * t + 128]))
    top = jnp.maximum(jnp.maximum(tops[0], tops[1]), tops[2])
    meta[0, 0] = top * (1.0 / LEVELS)
    inverse = LEVELS / jnp.maximum(top, 1e-30)
    for kind in range(PARTS):
        c, first = kind // EACH, kind % EACH * TILES
        for t in range(TILES):
            begin = 128 * (first + t)
            staged[kind][pl.ds(t, SLOTS, stride=TILES), :] = jnp.round(old[c, :, begin : begin + 128] * inverse)
        for b in range(SLOTS):
            codes = staged[kind][TILES * b : TILES * (b + 1), :]
            gathered[kind][b] = codes.astype(jnp.int32).astype(jnp.int16)
    label = jnp.zeros((8, 128), jnp.int32)
    for b in range(SLOTS):
        label = jnp.where(rows_of((8, 128)) == b, target[b], label)
    meta[0, 1] = label.astype(jnp.float32)

    pl.semaphore_wait(barrier, len(partners))

    def places(kind, place, count=8, skip=0):
        if kind == PARTS:
            return meta.at[pl.ds(place, count // 8)]
        return gathered[kind].at[pl.ds(8 * place + skip, count)]

    def hop_right(kind, hop):
        source = max(2 * hop - 3, 0)
        count = 4 if hop == 4 and kind < PARTS else 8
        send(("r", kind, hop), places(kind, source, count), places(kind, 2 * hop - 1, count), along("span", span, 1))

    def hop_left(kind, hop):
        source, to, count, skip = 2 * hop - 2, 2 * hop, 8, 0
        if hop == 4:
            to, count, skip = LAST, 4, 4
        send(("l", kind, hop), places(kind, source, count, skip), places(kind, to, count, skip), along("span", span, -1))

    def to_core(kind, hop):
        first = max(2 * hop - 1, 0)
        count = 8 if hop in (0, 4) else 16
        send(("c", kind, hop), places(kind, first, count), places(kind, 8 + first, count), other_core)

    kinds = (0, PARTS, *range(1, PARTS))
    for kind in kinds:
        hop_right(kind, 1)
        hop_left(kind, 1)
    for kind in kinds:
        to_core(kind, 0)

    wide, small = (EDGE, 128), (8, 128)
    lane, row, lane8, row8 = lanes_of(wide), rows_of(wide), lanes_of(small), rows_of(small)
    place8 = ((lane8 + 1) & 127) // 4
    after8 = (lane8 & 3) == 3
    odd8 = (place8 & 1) == 1

    def keep_row(n, i, c, y, layer, value):
        face_y[n][y][layer * 3 + c, i : i + 1, :] = value
        if layer == 0 and i in (0, EDGE - 1):
            corners[n][(i > 0) * 2 + y, c : c + 1, :] = value

    def keep_faces(n, i, c, value):
        for layer in (0, 1):
            keep_row(n, i, c, 0, layer, value[layer : layer + 1])
            keep_row(n, i, c, 1, layer, value[EDGE - 1 - layer : EDGE - layer])

    def start_faces(n, tiles):
        field = fields[n]
        for y in (1, 0):
            send(
                (n, "y", y),
                face_y[n][y].at[pl.ds(0, 3)],
                halo_y[n].at[1 - y, pl.ds(0, 3)],
                along("span", span, sides[y]),
            )
        for c in range(3):
            face_z[n][c] = pack_ends(tiles[c])
        for z in (0, 1):
            send((n, "z", z), face_z[n], halo_z[n].at[1 - z], along("depth", depth, sides[z]))
        send((n, "x", 1), field.at[pl.ds(51, 3)], field.at[pl.ds(3, 3)], along("stream", stream, 1))
        send((n, "x", 0), field.at[pl.ds(6, 3)], field.at[pl.ds(54, 3)], along("stream", stream, -1))

    def start_diagonals(n):
        field = fields[n]
        for x in (0, 1):
            for y in (0, 1):
                send(
                    (n, "xy", x, y),
                    corners[n].at[2 * x + y],
                    corners_in[n].at[3 - 2 * x - y],
                    diagonal("stream", sides[x], "span", sides[y]),
                )
        for number, axis in enumerate(("stream", "span")):
            for i in (0, 1):
                for z in (0, 1):
                    send(
                        (n, axis, i, z),
                        face_z[n],
                        edge_z[n].at[4 * number + 3 - 2 * i - z],
                        diagonal(axis, sides[i], "depth", sides[z]),
                    )
        for y in (1, 0):
            send(
                (n, "y2", y),
                face_y[n][y].at[pl.ds(3, 3)],
                halo_y[n].at[1 - y, pl.ds(3, 3)],
                along("span", span, sides[y]),
            )
        send((n, "x2", 1), field.at[pl.ds(48, 3)], field.at[pl.ds(0, 3)], along("stream", stream, 1))
        send((n, "x2", 0), field.at[pl.ds(9, 3)], field.at[pl.ds(57, 3)], along("stream", stream, -1))

    def ends(before, after, c, layer=1):
        low = jnp.where(depth == 0, 0.0, pltpu.roll(before[c], layer, 1))
        high = jnp.where(depth == RING - 1, 0.0, pltpu.roll(after[c], 128 - layer, 1))
        return jnp.where(after8, high, low)

    def finish_faces(n):
        for axis in ("x", "y", "z"):
            for side in (0, 1):
                copies[(n, axis, side)].wait_recv()
        for end, x in ((0, 0), (RING - 1, 1)):

            @pl.when(stream == end)
            def _():
                fields[n][3 + 51 * x : 6 + 51 * x] = jnp.zeros((3, EDGE, 128), jnp.float32)

            @pl.when(span == end)
            def _():
                halo_y[n][x, 0:3] = jnp.zeros((3, EDGE, 128), jnp.float32)

        return [ends(halo_z[n].at[0], halo_z[n].at[1], c) for c in range(3)]

    def finish_diagonals(n):
        for key in [key for key in copies if key[0] == n and key[1] not in ("x", "y", "z")]:
            copies[key].wait_recv()
        for end, x in ((0, 0), (RING - 1, 1)):

            @pl.when(stream == end)
            def _():
                fields[n][57 * x : 57 * x + 3] = jnp.zeros((3, EDGE, 128), jnp.float32)
                for y in (0, 1):
                    corners_in[n][2 * x + y] = jnp.zeros(small, jnp.float32)

            @pl.when(span == end)
            def _():
                halo_y[n][x, 3:6] = jnp.zeros((3, EDGE, 128), jnp.float32)
                for y in (0, 1):
                    corners_in[n][2 * y + x] = jnp.zeros(small, jnp.float32)

        second = [ends(halo_z[n].at[0], halo_z[n].at[1], c, 2) for c in range(3)]
        outside = (stream == 0, stream == RING - 1, span == 0, span == RING - 1)
        edges = [
            [
                jnp.where(outside[e], 0.0, ends(edge_z[n].at[2 * e], edge_z[n].at[2 * e + 1], c))
                for c in range(3)
            ]
            for e in range(4)
        ]
        return second, edges

    def around(planes, low, high, ends, first):
        before, here, after = planes
        y_before = jnp.where(row == 0, low, pltpu.roll(here, 1, 0))
        y_after = jnp.where(row == EDGE - 1, high, pltpu.roll(here, EDGE - 1, 0))
        end = jnp.concatenate(
            [pltpu.roll(ends, (128 - 4 * v) % 128, 1) for v in (first, first + 1)], axis=0
        )
        z_before = jnp.where(lane == 0, end, pltpu.roll(here, 1, 1))
        z_after = jnp.where(lane == 127, end, pltpu.roll(here, 127, 1))
        return before, after, y_before, y_after, z_before, z_after

    def plane_near(n, halo, i, c):
        beyond, _, edges = halo
        planes = [fields[n][(i + 1 + d) * 3 + c] for d in range(3)]
        if i < 0:
            low, high = (corners_in[n][y, c : c + 1, :] for y in (0, 1))
            return around(planes, low, high, edges[0][c], 30)
        if i == EDGE:
            low, high = (corners_in[n][2 + y, c : c + 1, :] for y in (0, 1))
            return around(planes, low, high, edges[1][c], 0)
        low, high = (halo_y[n][y, c, i : i + 1, :] for y in (0, 1))
        return around(planes, low, high, beyond[c], 2 * i)

    def row_near(n, halo, y, c):
        here, outer, inner = halo_y[n][y, c], halo_y[n][y, 3 + c], face_y[n][y][c]
        x_before = jnp.where(row == 0, corners_in[n][y, c : c + 1, :], pltpu.roll(here, 1, 0))
        x_after = jnp.where(row == EDGE - 1, corners_in[n][2 + y, c : c + 1, :], pltpu.roll(here, EDGE - 1, 0))
        edge = halo[2][2 + y][c][7 - 7 * y : 8 - 7 * y, :]
        columns = [
            jnp.sum(jnp.where(lane == ((8 * row + 4 - 4 * y - z) & 127), edge, 0.0), axis=1, keepdims=True)
            for z in (0, 1)
        ]
        z_before = jnp.where(lane == 0, columns[0], pltpu.roll(here, 1, 1))
        z_after = jnp.where(lane == 127, columns[1], pltpu.roll(here, 127, 1))
        y_pair = (inner, outer) if y else (outer, inner)
        return x_before, x_after, *y_pair, z_before, z_after

    def end_near(n, halo, c):
        here, outer, inner = halo[0][c], halo[1][c], face_z[n][c]
        x_low, x_high, y_low, y_high = (edge[c] for edge in halo[2])
        x_before = jnp.where(place8 < 2, pltpu.roll(x_low, 8, 1), pltpu.roll(here, 8, 1))
        x_after = jnp.where(place8 >= 30, pltpu.roll(x_high, 120, 1), pltpu.roll(here, 120, 1))
        into = jnp.where(odd8, pltpu.roll(here, 4, 1), pltpu.roll(y_low, 124, 1))
        y_before = jnp.where(row8 == 0, pltpu.roll(into, 1, 0), pltpu.roll(here, 1, 0))
        into = jnp.where(odd8, pltpu.roll(y_high, 4, 1), pltpu.roll(here, 124, 1))
        y_after = jnp.where(row8 == 7, pltpu.roll(into, 7, 0), pltpu.roll(here, 7, 0))
        z_before = jnp.where(after8, inner, outer)
        z_after = jnp.where(after8, outer, inner)
        return x_before, x_after, y_before, y_after, z_before, z_after

    fetched[1].wait()
    tiles = [[], [], []]
    for i in range(EDGE):
        for c in range(3):
            value = velocity[c, i].astype(jnp.float32)
            fields[2][(i + 2) * 3 + c] = value
            keep_faces(2, i, c, value)
            tiles[c] += [value[0:8], value[8:16]]
    start_faces(2, tiles)

    def forward(kind, hop):
        copies[("r", kind, hop)].wait_recv()
        if hop < 4:
            hop_right(kind, hop + 1)
        if hop < 4 or kind < PARTS:
            copies[("l", kind, hop)].wait_recv()
        if hop < 3 or hop == 3 and kind < PARTS:
            hop_left(kind, hop + 1)
        to_core(kind, hop)

    for kind in kinds:
        forward(kind, 1)

    for kind in kinds:
        forward(kind, 2)
    beyond = finish_faces(2)
    start_diagonals(2)

    for kind in kinds:
        forward(kind, 3)
    for kind in (PARTS, *range(PARTS // 2)):
        forward(kind, 4)
    for hop in range(5):
        copies[("c", PARTS, hop)].wait_recv()

    owner = (2 * ((chip + lane8 // 8) % CHIPS) + core) * RING + span
    wanted = jnp.where(lane8 < CHIPS * SLOTS, owner * SLOTS + lane8 % 8, -1).astype(jnp.float32)
    at = jnp.zeros(small, jnp.float32)
    for e in range(16):
        at = at + jnp.where(meta[e, 1] == wanted, (row8 + (8 * e + 1)).astype(jnp.float32), 0.0)
    found[...] = jnp.broadcast_to(jnp.sum(at, axis=0, keepdims=True), small).astype(jnp.int32)
    copy = pltpu.make_async_copy(found, found_s, local_sems.at[3])
    copy.start()
    copy.wait()
    where_from = []
    for q in range(CHIPS * SLOTS):
        k, j = q // SLOTS, q % SLOTS
        code = found_s[0, q]
        block = jnp.minimum(jnp.maximum(code - 1, 0), 127)
        where_from.append(block)
        scale = meta[block >> 3, 0, pl.ds(block & 7, 1), :] * jnp.where(code > 0, 1.0, 0.0)
        if k == 0:
            in_scales[0, j : j + 1, :] = scale
        else:
            out_scales[k - 1, j : j + 1, :] = scale
    for k in (2, 1, 3):
        send(("s", k), out_scales.at[k - 1], in_scales.at[k], along("stream", stream, 2 * k))

    def pick(kind):
        for hop in range(5):
            copies[("c", kind, hop)].wait_recv()
        for k in (2, 1, 3, 0):
            for j in range(SLOTS):
                block = gathered[kind][where_from[k * SLOTS + j]]
                if k == 0:
                    incoming[kind][0, j] = block
                else:
                    outgoing[kind][k - 1, j] = block
            if k:
                send(("x", kind, k), outgoing[kind].at[k - 1], incoming[kind].at[k], along("stream", stream, 2 * k))

    for kind in range(PARTS):
        pick(kind)
        for later in range(PARTS // 2, PARTS) if kind == 0 else ():
            forward(later, 4)

    fetched[2].wait()
    group = lane // EDGE
    forces = []
    for c in range(3):
        force = jnp.zeros(wide, jnp.float32)
        for b in range(SLOTS):
            force = jnp.where(group == b, forcing[c, fish[0, 0, b]], force)
        forces.append(force)
    for i in range(EDGE):
        level = chi[i]
        share = 1.0 / (1.0 + level)
        weight[i] = share
        for c in range(3):
            pull[i * 3 + c] = level * share * forces[c]

    halo = (beyond, *finish_diagonals(2))
    for k in range(3):
        carried_z[k] = ADVECT * halo[0][k]
        beside_ends = end_near(2, halo, k)
        beside_rows = [row_near(2, halo, y, k) for y in (0, 1)]
        for axis in range(3):
            slopes_z[axis * 3 + k] = ADVECT * (beside_ends[2 * axis + 1] - beside_ends[2 * axis])
            for y in (0, 1):
                slopes_y[y * 9 + axis * 3 + k] = ADVECT * (beside_rows[y][2 * axis + 1] - beside_rows[y][2 * axis])
    for i in range(-1, EDGE + 1):
        for k in range(3):
            near = plane_near(2, halo, i, k)
            for axis in range(3):
                slopes[(axis * 3 + k) * 18 + i + 1] = ADVECT * (near[2 * axis + 1] - near[2 * axis])


    for k in (2, 1, 3):
        copies[("s", k)].wait_recv()
    tiles = [[], [], []]
    for kind in range(PARTS):
        c, first = kind // EACH, kind % EACH * (EDGE // EACH)
        for k in (2, 1, 3):
            copies[("x", kind, k)].wait_recv()
        for j in range(SLOTS):
            total = incoming[kind][0, j].astype(jnp.float32) * in_scales[0, j : j + 1, :]
            for k in range(1, CHIPS):
                total = total + incoming[kind][k, j].astype(jnp.float32) * in_scales[k, j : j + 1, :]
            decoded[kind][TILES * j : TILES * (j + 1), :] = total
        moved = swap_groups([decoded[kind][pl.ds(t, SLOTS, stride=TILES), :] for t in range(TILES)])
        tiles[c] += moved
        for t, tile in enumerate(moved):
            i, h = first + t // 2, t % 2
            fields[0][(i + 2) * 3 + c, 8 * h : 8 * h + 8, :] = tile
            for layer in (0, 1):
                at = 7 - layer if h else layer
                keep_row(0, i, c, h, layer, tile[at : at + 1])

    settled = set()
    for section in range(SECTIONS):
        sent = [copy for key, copy in copies.items() if key not in settled]
        settled.update(copies)
        start_faces(section, tiles)
        start_diagonals(section)
        for copy in sent:
            copy.wait_send()
        beyond = finish_faces(section)
        halo = (beyond, None, None)
        for i in (*range(EDGE), -1, EDGE):
            if i < 0:
                halo = (beyond, *finish_diagonals(section))
            here = [fields[section][(i + 2) * 3 + c] for c in range(3)]
            near = [plane_near(section, halo, i, c) for c in range(3)]
            carried = [ADVECT * fields[2][(i + 2) * 3 + k] for k in range(3)]
            values = advected(here, near, carried, lambda c, k: slopes[(c * 3 + k) * 18 + i + 1])
            for c in range(3):
                value = values[c]
                if i in (-1, EDGE):
                    value = jnp.where(stream == (0 if i < 0 else RING - 1), 0.0, value)
                moved_x[(i + 1) * 3 + c] = value
        here = beyond
        near = [end_near(section, halo, c) for c in range(3)]
        values = advected(here, near, [carried_z[k] for k in range(3)], lambda c, k: slopes_z[c * 3 + k])
        for c in range(3):
            moved_z[c] = jnp.where(jnp.where(after8, RING - 1, 0) == depth, 0.0, values[c])
        for y in (0, 1):
            here = [halo_y[section][y, c] for c in range(3)]
            near = [row_near(section, halo, y, c) for c in range(3)]
            carried = [ADVECT * halo_y[2][y, k] for k in range(3)]
            values = advected(here, near, carried, lambda c, k: slopes_y[y * 9 + c * 3 + k])
            for c in range(3):
                moved_y[y * 3 + c] = jnp.where(span == (RING - 1) * y, 0.0, values[c])
        tiles = [[], [], []]
        for i in range(EDGE):
            share = weight[i]
            for c in range(3):
                planes = [moved_x[(i + d) * 3 + c] for d in range(3)]
                low, high = (moved_y[y * 3 + c, i : i + 1, :] for y in (0, 1))
                near = around(planes, low, high, moved_z[c], 2 * i)
                total = (near[0] + near[1]) + (near[2] + near[3]) + (near[4] + near[5])
                value = (planes[1] + DIFFUSE * (total - 6.0 * planes[1])) * share + pull[i * 3 + c]
                if section == SECTIONS - 1:
                    out[c, i] = value
                else:
                    fields[section + 1][(i + 2) * 3 + c] = value
                    keep_faces(section + 1, i, c, value)
                    tiles[c] += [value[0:8], value[8:16]]

    for key, copy in copies.items():
        if key not in settled:
            copy.wait_send()


def body(old_adjoint, target, velocity, chi, fish, fish_forcing):
    f32, i16 = jnp.float32, jnp.int16
    v = pltpu.VMEM
    scratch = [
        v((3, SLOTS, EACH * TILES * 128), f32),
        v(velocity.shape, velocity.dtype),
        v(chi.shape, f32),
        [v((128, TILES, 128), i16)] * PARTS,
        v((16, 2, 8, 128), f32),
        [v((SLOTS * TILES, 128), f32)] * PARTS,
        [v((CHIPS - 1, SLOTS, TILES, 128), i16)] * PARTS,
        v((CHIPS - 1, SLOTS, 128), f32),
        [v((CHIPS, SLOTS, TILES, 128), i16)] * PARTS,
        v((CHIPS, SLOTS, 128), f32),
        [v((SLOTS * TILES, 128), f32)] * PARTS,
        v((8, 128), jnp.int32),
        pltpu.SMEM((8, 128), jnp.int32),
        [v((20 * 3, EDGE, 128), f32)] * 3,
        [[v((6, EDGE, 128), f32)] * 2] * 3,
        [v((2, 6, EDGE, 128), f32)] * 3,
        [v((3, 8, 128), f32)] * 3,
        [v((2, 3, 8, 128), f32)] * 3,
        [v((4, 8, 128), f32)] * 3,
        [v((4, 8, 128), f32)] * 3,
        [v((8, 3, 8, 128), f32)] * 3,
        v((18 * 3, EDGE, 128), f32),
        v((6, EDGE, 128), f32),
        v((3, 8, 128), f32),
        v((9 * 18, EDGE, 128), f32),
        v((18, EDGE, 128), f32),
        v((9, 8, 128), f32),
        v((3, 8, 128), f32),
        v((EDGE, EDGE, 128), f32),
        v((3 * EDGE, EDGE, 128), f32),
        pltpu.SemaphoreType.DMA((192,)),
        pltpu.SemaphoreType.DMA((192,)),
        pltpu.SemaphoreType.DMA((4,)),
    ]
    smem = pl.BlockSpec(memory_space=pltpu.SMEM)
    far = pl.BlockSpec(memory_space=pl.ANY)
    vmem = pl.BlockSpec(memory_space=pltpu.VMEM)
    return pl.pallas_call(
        kernel,
        out_shape=jax.ShapeDtypeStruct(velocity.shape, f32),
        in_specs=[smem, smem, smem, far, far, far],
        out_specs=vmem,
        scratch_shapes=scratch,
        compiler_params=pltpu.CompilerParams(
            collective_id=0, has_side_effects=True, vmem_limit_bytes=63 * 1024 * 1024
        ),
    )(target, fish, fish_forcing.T, old_adjoint, velocity, chi)


def solution(mesh):
    return jax.shard_map(
        body,
        mesh=mesh,
        in_specs=(
            P(None, ("stream", "span", "depth"), None),
            P(("stream", "span", "depth")),
            P(None, "stream", "span", "depth"),
            P("stream", "span", "depth"),
            P("stream", "span", "depth"),
            P(),
        ),
        out_specs=P(None, "stream", "span", "depth"),
        check_vma=False,
    )
```
